32 devices in a mesh: dp: 8 (over y, x, core), mp: 4 (over z).
Axes of the slice: x: 2, y: 2, z: 4, core: 2. Of those that a mesh axis runs over, the one named last changes fastest.
Arguments:
- residual_in: bfloat16 [8192, 1024], P(('dp', 'mp')), may hold values from -6 to 6
- upstream: bfloat16 [8192, 1024], P(('dp', 'mp')), may hold values from -6 to 6
- layer_norm_gain: float32 [1024], replicated, may hold values from 0.1 to 1.9
- layer_norm_bias: float32 [1024], replicated, may hold values from -3 to 3
- attend_weight: bfloat16 [1024, 3072], replicated, may hold values from -0.1875 to 0.1875
- output_weight: bfloat16 [1024, 1024], replicated, may hold values from -1 to 1
- expand_weight: bfloat16 [1024, 4096], P(None, 'mp'), may hold values from -0.1875 to 0.1875
- expand_bias: float32 [4096], P('mp'), may hold values from -3 to 3
- shrink_weight: bfloat16 [4096, 1024], P('mp'), may hold values from -0.09375 to 0.09375
- shrink_bias: float32 [1024], replicated, may hold values from -3 to 3
- seq_lengths: int32 [8, 16], P('dp'), may hold values from 0 to 256, as said below
- terminal_pos: int32 [8, 16], P('dp', 'mp'), may hold values from 0 to 255, as said below
- window_offset: int32 [8, 16], P('dp', 'mp'), may hold values from 0 to 8191
Outputs:
- residual_out: bfloat16 [8192, 1024], P(('dp', 'mp'))
- residual_grad: float32 [8192, 1024], P(('dp', 'mp'))
- norm_gain_gradient: float32 [1024], replicated
- shift_grad: float32 [1024], replicated
- attend_grad: float32 [1024, 3072], P('dp')
- output_grad: float32 [1024, 1024], P('dp')
- expand_grad: float32 [1024, 4096], P('dp', 'mp')
- expand_bias_grad: float32 [4096], P('mp')
- shrink_grad: float32 [4096, 1024], P('mp', 'dp')
- shrink_bias_grad: float32 [1024], replicated
The draws below stay inside these ranges and needn't reach their ends.
Inputs may be any that keep to these rules, and one draw needn't show every extreme that they name: `seq_lengths`: the lengths of one device's 4 slots sum to at most 256; its sequences fill its rows from the first in slot order and the remaining rows are padding; an empty slot has length 0. `terminal_pos`: below the slot's length; 0 for an empty slot.
All inputs are finite; a program needn't handle non-finite values.
Results may differ from the reference program's by a relative error of at most 0.015.
Values may be sent and summed in bfloat16 or wider, within the bound.
No kernel may reach another device: no remote copies, remote signals or barrier semaphores. Data moves between devices by JAX's collectives and lax.ppermute only.
A program may use at most 128 MiB of HBM per device.

```python
import jax
import jax.numpy as jnp
from jax import lax

D = 1024
HEADS = 16
HEAD_DIM = 64
ROT = 32
FF = 4096
TOK_DEV = 256
SEQ_DEV = 4
TOKENS = 8192
SLOTS = 16
N_DP = 8
N_MP = 4


def layout_draw(key):
    group = jnp.arange(N_DP, dtype=jnp.int32)[:, None]
    slot = jnp.arange(N_MP * SEQ_DEV, dtype=jnp.int32)[None, :]
    device = slot // SEQ_DEV
    within = slot % SEQ_DEV
    live_slots = SEQ_DEV - group * SEQ_DEV // N_DP
    target = TOK_DEV * (N_DP - 1 + 2 * group) // (3 * (N_DP - 1))
    upper = target // live_slots
    lowest = upper // 2
    raw_length = jax.random.randint(jax.random.fold_in(key, 11), (N_DP, N_MP * SEQ_DEV), 0, 1 << 20)
    length = lowest + raw_length % (upper - lowest + 1)
    length = jnp.where(within < live_slots, length, 0)
    top_device = (group == N_DP - 1) & (device == 0)
    forced = top_device & (within == 0)
    length = jnp.where(top_device & (within > 0), 0, length)
    length = jnp.where(forced, TOK_DEV, length)
    raw_end = jax.random.randint(jax.random.fold_in(key, 12), (N_DP, N_MP * SEQ_DEV), 0, 1 << 20)
    terminal = raw_end % jnp.maximum(length, 1)
    terminal = jnp.where(forced, TOK_DEV - 1, terminal)
    return (length.astype(jnp.int32), terminal.astype(jnp.int32))


def draw_seq_lengths(key, part):
    return layout_draw(key)[0]


def draw_terminal_pos(key, part):
    return layout_draw(key)[1]


def plant(entries, key, smallest, high):
    index_at = [jax.random.randint(jax.random.fold_in(key, axis), (), 0, length) for axis, length in enumerate(entries.shape)]
    widest = entries.shape.index(max(entries.shape))
    next_to = index_at[:widest] + [(index_at[widest] + 1) % entries.shape[widest]] + index_at[widest + 1:]
    return entries.at[tuple(index_at)].set(smallest).at[tuple(next_to)].set(high)


def block_levels(own_key, dims, pieces, smallest, top_value):
    level = 1.0
    for dim, blocks in pieces:
        steps = jax.random.uniform(jax.random.fold_in(jax.random.fold_in(own_key, 6), dim), (blocks,), jnp.float32, smallest / len(pieces), top_value / len(pieces))
        level = level * jnp.repeat(jnp.exp(steps), dims[dim] // blocks).reshape((-1,) + (1,) * (len(dims) - 1 - dim))
    return level


def normal_values(rng, extent, width, bound, shards=(), held_as=jnp.bfloat16):
    drawn = jax.random.normal(rng, extent, jnp.float32) * width
    if len(shards) > 0:
        drawn = block_levels(rng, extent, shards, -0.22, 0.18) * drawn
    return jnp.clip(drawn, min=-bound, max=bound).astype(held_as)


def setup_inputs(seed: int = 0) -> dict:
    splits = jax.random.split(jax.random.key(seed), 14)
    residual_in = normal_values(splits[0], (TOKENS, D), 1.0, 6.0, ((0, 32),))
    upstream = normal_values(splits[1], (TOKENS, D), 1.0, 6.0, ((0, 32),))
    layer_norm_gain = jnp.clip(1.0 + 0.18 * jax.random.normal(splits[2], (D,), jnp.float32), 0.1, 1.9)
    layer_norm_bias = normal_values(splits[3], (D,), 0.5, 3.0, (), jnp.float32)
    attend_weight = normal_values(splits[4], (D, 3 * D), D ** -0.5, 0.1875)
    output_weight = normal_values(splits[5], (D, D), (D // 32) ** -0.5, 1.0)
    expand_weight = normal_values(splits[6], (D, FF), D ** -0.5, 0.1875, ((1, 4),))
    expand_bias = normal_values(splits[7], (FF,), 0.5, 3.0, ((0, 4),), jnp.float32)
    shrink_weight = normal_values(splits[8], (FF, D), FF ** -0.5, 0.09375, ((0, 4),))
    shrink_bias = normal_values(splits[9], (D,), 0.5, 3.0, (), jnp.float32)
    seq_lengths = draw_seq_lengths(jax.random.fold_in(splits[13], 71), 0)
    terminal_pos = draw_terminal_pos(jax.random.fold_in(splits[13], 71), 0)
    window_offset = plant(jax.random.randint(splits[12], (N_DP, SLOTS), 0, 8192), jax.random.fold_in(splits[12], 1), 0, 8191).astype(jnp.int32)
    return {"residual_in": residual_in, "upstream": upstream, "layer_norm_gain": layer_norm_gain, "layer_norm_bias": layer_norm_bias, "attend_weight": attend_weight, "output_weight": output_weight, "expand_weight": expand_weight, "expand_bias": expand_bias, "shrink_weight": shrink_weight, "shrink_bias": shrink_bias, "seq_lengths": seq_lengths, "terminal_pos": terminal_pos, "window_offset": window_offset}


@jax.custom_vjp
def low(v):
    return lax.optimization_barrier(v.astype(jnp.bfloat16)).astype(jnp.float32)

@jax.custom_vjp
def low_back(v):
    return v

def low_keep(v):
    return (low(v), None)

def low_pass(kept, grad):
    return (grad,)

def back_keep(v):
    return (v, None)

def back_low(kept, grad):
    return (low(grad),)
low.defvjp(low_keep, low_pass)
low_back.defvjp(back_keep, back_low)
EPSILON = 1e-05
HIGH = lax.Precision.HIGHEST

def layout(lengths_row, terminal_row, offset_row):
    seq_ends = jnp.cumsum(lengths_row).astype(jnp.int32)
    seq_starts = (seq_ends - lengths_row).astype(jnp.int32)
    places = jnp.arange(TOK_DEV, dtype=jnp.int32)
    seq_index = lax.optimization_barrier(jnp.sum((places[:, None] >= seq_ends[None, :]).astype(jnp.int32), axis=1)).astype(jnp.int32)
    member = seq_index[:, None] == jnp.arange(SEQ_DEV, dtype=jnp.int32)[None, :]
    local_index = (places - lax.optimization_barrier(jnp.sum(jnp.where(member, seq_starts[None, :], 0), axis=1))).astype(jnp.int32)
    terminal = lax.optimization_barrier(jnp.sum(jnp.where(member, terminal_row[None, :], 0), axis=1)).astype(jnp.int32)
    offset = lax.optimization_barrier(jnp.sum(jnp.where(member, offset_row[None, :], 0), axis=1)).astype(jnp.int32)
    positions = jnp.where(local_index <= terminal, offset + local_index, local_index - terminal - 1)
    live_rows = (seq_index < SEQ_DEV).astype(jnp.float32)
    return (seq_index, positions.astype(jnp.float32), live_rows)

def rotary_tables(positions):
    pair_index = jnp.arange(HEAD_DIM, dtype=jnp.int32) // 2
    frequency = jnp.where(pair_index < ROT // 2, 10000.0 ** (-2.0 * pair_index.astype(jnp.float32) / ROT), 0.0)
    angles = positions[:, None] * frequency[None, :]
    parity = jnp.arange(HEAD_DIM, dtype=jnp.int32) % 2
    return (jnp.cos(angles), jnp.where(parity == 0, -jnp.sin(angles), jnp.sin(angles)))

def rotate(values, cosine, signed_sine):
    shape = values.shape
    swapped = values.reshape(shape[0], shape[1], shape[2] // 2, 2)[..., ::-1].reshape(shape)
    return values * cosine[:, None, :] + swapped * signed_sine[:, None, :]

def device_layer(params, hidden, seq_index, positions, live_rows):
    gain, shift, attend_w, output_w, expand_w, expand_b, shrink_w, shrink_b = params
    tokens = hidden.shape[0]
    row_mean = lax.optimization_barrier(jnp.mean(hidden, axis=-1, keepdims=True))
    mean_removed = hidden - row_mean
    variance = lax.optimization_barrier(jnp.mean(mean_removed * mean_removed, axis=-1, keepdims=True))
    normed = low(mean_removed * lax.rsqrt(variance + EPSILON) * gain + shift)
    projected = low_back(jnp.dot(normed, attend_w, precision=HIGH))
    query_part = projected[:, :D].reshape(tokens, HEADS, HEAD_DIM)
    key_part = projected[:, D:2 * D].reshape(tokens, HEADS, HEAD_DIM)
    value_part = projected[:, 2 * D:].reshape(tokens, HEADS, HEAD_DIM)
    cosine, signed_sine = rotary_tables(positions)
    queries = low(rotate(query_part, cosine, signed_sine) * HEAD_DIM ** (-0.5))
    key_rows = low(rotate(key_part, cosine, signed_sine))
    value_rows = low(value_part)
    scores = low_back(jnp.einsum('qhd,khd->hqk', queries, key_rows, precision=HIGH))
    places = jnp.arange(tokens, dtype=jnp.int32)
    allowed = (seq_index[None, :] == seq_index[:, None]) & (places[None, :] <= places[:, None])
    scores = jnp.where(allowed[None], scores, -1e+30)
    row_max = lax.optimization_barrier(jnp.max(scores, axis=-1, keepdims=True))
    exponent = jnp.exp(scores - row_max)
    probs = low(exponent / lax.optimization_barrier(jnp.sum(exponent, axis=-1, keepdims=True)))
    attended = jnp.einsum('hqk,khd->qhd', probs, value_rows, precision=HIGH).reshape(tokens, D)
    attended = low(low_back(attended))
    attention_out = jnp.dot(attended, output_w, precision=HIGH)
    expanded = low_back(jnp.dot(normed, expand_w, precision=HIGH) + expand_b)
    activated = low(jax.nn.gelu(expanded, approximate=True))
    partials = jnp.einsum('tmf,mfd->tmd', activated.reshape(tokens, N_MP, FF // N_MP), shrink_w.reshape(N_MP, FF // N_MP, D), precision=HIGH)
    mlp_out = lax.optimization_barrier(jnp.sum(low(partials), axis=1)) + shrink_b
    branch = low_back(attention_out + mlp_out)
    return hidden + live_rows[:, None] * branch

def reference(residual_in, upstream, layer_norm_gain, layer_norm_bias, attend_weight, output_weight, expand_weight, expand_bias, shrink_weight, shrink_bias, seq_lengths, terminal_pos, window_offset):
    devices_all = N_DP * N_MP
    params = tuple((item.astype(jnp.float32) for item in (layer_norm_gain, layer_norm_bias, attend_weight, output_weight, expand_weight, expand_bias, shrink_weight, shrink_bias)))
    hidden = residual_in.astype(jnp.float32).reshape(devices_all, TOK_DEV, D)
    lengths_dev = seq_lengths.reshape(devices_all, SEQ_DEV)
    terminal_dev = terminal_pos.reshape(devices_all, SEQ_DEV)
    offset_dev = window_offset.reshape(devices_all, SEQ_DEV)
    seq_index, positions, live_rows = jax.vmap(layout)(lengths_dev, terminal_dev, offset_dev)

    def forward(weights, inputs):

        def one_device(items):
            return device_layer(weights, items[0], items[1], items[2], items[3])
        return lax.map(jax.checkpoint(one_device), (inputs, seq_index, positions, live_rows))
    result, pullback = jax.vjp(forward, params, hidden)
    counts = lax.optimization_barrier(jnp.sum(seq_lengths, axis=1)).astype(jnp.float32)
    group_weight = N_DP * counts / jnp.sum(counts)
    scaled = upstream.astype(jnp.float32).reshape(N_DP, N_MP * TOK_DEV, D) * group_weight[:, None, None]
    param_grads, hidden_grad = pullback(scaled.reshape(devices_all, TOK_DEV, D))
    return (result.reshape(TOKENS, D).astype(jnp.bfloat16), hidden_grad.reshape(TOKENS, D), param_grads[0], param_grads[1], param_grads[2], param_grads[3], param_grads[4], param_grads[5], param_grads[6], param_grads[7])
```

```python
from functools import partial

import numpy as np

import jax
import jax.numpy as jnp
from jax import lax
from jax.experimental import pallas as pl
from jax.experimental.pallas import tpu as pltpu
from jax.sharding import PartitionSpec as P

HEADS = 16
HEAD_DIM = 64
ROT = 32
SEQ_DEV = 4
EPSILON = 1e-05
NEGATIVE = -1e30
LANES = 256
BF = jnp.bfloat16
F32 = jnp.float32
MIB = 1 << 20

CORE, CHIP, ZPOS, LIVE, COUNT, LENS, TERMS, OFFS = 0, 1, 2, 3, 4, 5, 9, 13


def nn(a, b):
    return lax.dot_general(a, b, (((1,), (0,)), ((), ())), preferred_element_type=F32)


def nt(a, b):
    return lax.dot_general(a, b, (((1,), (1,)), ((), ())), preferred_element_type=F32)


def call(kernel, meta, args, in_specs, outs, out_specs, scratch=(), grid=(1,), vmem=40, flops=0):
    moved = sum(int(np.prod(a.shape)) * a.dtype.itemsize for a in (*args, *jax.tree.leaves(outs)))
    return pl.pallas_call(
        kernel,
        grid_spec=pltpu.PrefetchScalarGridSpec(
            num_scalar_prefetch=1,
            grid=grid,
            in_specs=in_specs,
            out_specs=out_specs,
            scratch_shapes=list(scratch),
        ),
        out_shape=outs,
        compiler_params=pltpu.CompilerParams(vmem_limit_bytes=vmem * MIB),
        cost_estimate=pl.CostEstimate(flops=flops, bytes_accessed=moved, transcendentals=0),
    )(meta, *args)


def whole(shape):
    return pl.BlockSpec(shape, lambda i, meta: (0,) * len(shape))


ANY = pl.BlockSpec(memory_space=pl.ANY)


def struct(shape, dtype):
    return jax.ShapeDtypeStruct(shape, dtype)


def normalize(hidden):
    mean = jnp.mean(hidden, axis=-1, keepdims=True)
    removed = hidden - mean
    variance = jnp.mean(removed * removed, axis=-1, keepdims=True)
    inverse = lax.rsqrt(variance + EPSILON)
    return removed * inverse, inverse


def prepare_kernel(meta, x_ref, u_ref, gain_ref, bias_ref, tok_ref, sum_ref):
    rows, width = x_ref.shape
    step = 64
    live = meta[LIVE]
    count = meta[COUNT].astype(F32)
    total = jnp.zeros((1, width), F32)
    for r in range(0, rows, step):
        xhat, _ = normalize(x_ref[r : r + step, :].astype(F32))
        tok_ref[r : r + step, :] = (xhat * gain_ref[...] + bias_ref[...]).astype(BF)
        place = lax.broadcasted_iota(jnp.int32, (step, width), 0) + r
        grad = jnp.where(place < live, u_ref[r : r + step, :].astype(F32) * count, 0.0).astype(BF)
        tok_ref[rows + r : rows + r + step, :] = grad
        total = total + jnp.sum(grad.astype(F32), axis=0, keepdims=True)
    sum_ref[...] = total


def prepare(meta, x, u, gain, bias):
    rows, width = x.shape
    return call(
        prepare_kernel,
        meta,
        (x, u, gain, bias),
        [whole(x.shape), whole(x.shape), whole((1, width)), whole((1, width))],
        (struct((2 * rows, width), BF), struct((1, width), F32)),
        (whole((2 * rows, width)), whole((1, width))),
        vmem=16,
        flops=20 * rows * width,
    )


def slot_of(place, ends):
    index = jnp.zeros(place.shape, jnp.int32)
    for end in ends:
        index = index + (place >= end).astype(jnp.int32)
    return index


def attention_kernel(
    meta, tok_ref, freq_ref, wq_ref, wk_ref, wv_ref, wo_ref, out_ref, cos_ref, sin_ref, mask_ref
):
    rows = cos_ref.shape[0]
    lanes = cos_ref.shape[1]

    @pl.when(pl.program_id(0) == 0)
    def tables():
        ends, starts, end = [], [], 0
        for s in range(SEQ_DEV):
            starts.append(end)
            end = end + meta[LENS + s]
            ends.append(end)
        place = lax.broadcasted_iota(jnp.int32, (rows, lanes), 0)
        index = slot_of(place, ends)
        start = jnp.zeros(place.shape, jnp.int32)
        terminal = jnp.zeros(place.shape, jnp.int32)
        offset = jnp.zeros(place.shape, jnp.int32)
        for s in range(SEQ_DEV):
            here = index == s
            start = jnp.where(here, starts[s], start)
            terminal = jnp.where(here, meta[TERMS + s], terminal)
            offset = jnp.where(here, meta[OFFS + s], offset)
        local = place - start
        position = jnp.where(local <= terminal, offset + local, local - terminal - 1)
        angle = position.astype(F32) * freq_ref[...]
        parity = lax.broadcasted_iota(jnp.int32, (rows, lanes), 1) % 2
        sine = jnp.sin(angle)
        cos_ref[...] = jnp.cos(angle)
        sin_ref[...] = jnp.where(parity == 0, -sine, sine)
        key = lax.broadcasted_iota(jnp.int32, (rows, rows), 0)
        query = lax.broadcasted_iota(jnp.int32, (rows, rows), 1)
        allowed = (slot_of(key, ends) == slot_of(query, ends)) & (key <= query)
        mask_ref[...] = jnp.where(allowed, 0.0, NEGATIVE)

    even = lax.broadcasted_iota(jnp.int32, (rows, lanes), 1) % 2 == 0

    def swap(v):
        return jnp.where(even, pltpu.roll(v, lanes - 1, 1), pltpu.roll(v, 1, 1))

    def turn(v):
        return v * cos_ref[...] + swap(v) * sin_ref[...]

    def turn_back(v):
        return v * cos_ref[...] - swap(v) * sin_ref[...]

    scale = HEAD_DIM ** (-0.5)
    normed = tok_ref[:rows, :]
    queries = (turn(nn(normed, wq_ref[...])) * scale).astype(BF)
    keys = turn(nn(normed, wk_ref[...])).astype(BF)
    values = nn(normed, wv_ref[...]).astype(BF)
    grads = nt(tok_ref[rows:, :], wo_ref[...]).astype(BF)
    keys_t = keys.T
    values_t = values.T
    pair = 2 * HEAD_DIM
    lane = lax.broadcasted_iota(jnp.int32, (rows, pair), 1)
    attended_t, query_grad_t, key_grads, value_grads = [], [], [], []
    for p in range(lanes // pair):
        cols = slice(p * pair, (p + 1) * pair)
        q2, k2, v2, g2 = queries[:, cols], keys[:, cols], values[:, cols], grads[:, cols]
        key_grad = jnp.zeros((rows, pair), F32)
        value_grad = jnp.zeros((rows, pair), F32)
        for h in range(2):
            mine = (lane >= h * HEAD_DIM) & (lane < (h + 1) * HEAD_DIM)
            qh = jnp.where(mine, q2, jnp.zeros_like(q2))
            gh = jnp.where(mine, g2, jnp.zeros_like(g2))
            head = slice(p * pair + h * HEAD_DIM, p * pair + (h + 1) * HEAD_DIM)
            scores = nt(k2, qh) + mask_ref[...]
            exponent = jnp.exp(scores - jnp.max(scores, axis=0, keepdims=True))
            probs = exponent / jnp.sum(exponent, axis=0, keepdims=True)
            probs_low = probs.astype(BF)
            attended_t.append(nn(values_t[head, :], probs_low))
            probs_grad = nt(v2, gh)
            row_dot = jnp.sum(probs * probs_grad, axis=0, keepdims=True)
            scores_grad = (probs * (probs_grad - row_dot)).astype(BF)
            query_grad_t.append(nn(keys_t[head, :], scores_grad))
            key_grad = key_grad + nn(scores_grad, qh)
            value_grad = value_grad + nn(probs_low, gh)
        key_grads.append(key_grad)
        value_grads.append(value_grad)
    out_ref[0] = jnp.concatenate(attended_t, axis=0).T.astype(BF)
    out_ref[1] = turn_back(jnp.concatenate(query_grad_t, axis=0).T * scale).astype(BF)
    out_ref[2] = turn_back(jnp.concatenate(key_grads, axis=1)).astype(BF)
    out_ref[3] = jnp.concatenate(value_grads, axis=1).astype(BF)


def attention(meta, tok, attend_weight, output_weight):
    rows, width = tok.shape[0] // 2, tok.shape[1]
    blocks = width // LANES
    pair = np.arange(LANES) % HEAD_DIM // 2
    freq = np.where(pair < ROT // 2, 10000.0 ** (-2.0 * pair / ROT), 0.0)[None].astype(np.float32)
    column = lambda p: pl.BlockSpec((width, LANES), lambda i, meta: (0, p * blocks + i))
    return call(
        attention_kernel,
        meta,
        (tok, jnp.asarray(freq), attend_weight, attend_weight, attend_weight, output_weight),
        [
            whole(tok.shape),
            whole((1, LANES)),
            column(0),
            column(1),
            column(2),
            pl.BlockSpec((LANES, width), lambda i, meta: (i, 0)),
        ],
        struct((4, rows, width), BF),
        pl.BlockSpec((4, rows, LANES), lambda i, meta: (0, 0, i)),
        scratch=[
            pltpu.VMEM((rows, LANES), F32),
            pltpu.VMEM((rows, LANES), F32),
            pltpu.VMEM((rows, rows), F32),
        ],
        grid=(blocks,),
        flops=2 * rows * width * (4 * width + 7 * rows * 4),
    )


def attention_back_kernel(meta, sb_ref, wa_ref, wo_ref, grad_ref, out_ref):
    width = sb_ref.shape[2]
    grad = nt(sb_ref[1], wa_ref[:, :width])
    grad = grad + nt(sb_ref[2], wa_ref[:, width : 2 * width])
    grad_ref[...] = grad + nt(sb_ref[3], wa_ref[:, 2 * width :])
    out_ref[...] = nn(sb_ref[0], wo_ref[...])


def attention_back(meta, sb, attend_weight, output_weight):
    _, rows, width = sb.shape
    block = pl.BlockSpec((rows, LANES), lambda i, meta: (0, i))
    return call(
        attention_back_kernel,
        meta,
        (sb, attend_weight, output_weight),
        [
            whole(sb.shape),
            pl.BlockSpec((LANES, 3 * width), lambda i, meta: (i, 0)),
            pl.BlockSpec((width, LANES), lambda i, meta: (0, i)),
        ],
        (struct((rows, width), F32), struct((rows, width), F32)),
        (block, block),
        grid=(width // LANES,),
        flops=8 * rows * width * width,
    )


def with_bit(n, bit):
    return [j for j in range(n) if j >> bit & 1]


def without_bit(n, bit):
    return [j for j in range(n) if not j >> bit & 1]


def attention_grads_kernel(chips, depth, meta, t0, t1, s0, s1, ps, pk, qs, qk, ln, la, acc, sem):
    rows, width = s0.shape[1:]
    chunk = width // chips
    half = chunk // 2
    cols = 4 * width // depth
    core = meta[CORE]
    for s, (tok, sb) in enumerate(((t0, s0), (t1, s1))):
        for k in range(chips):
            for ref, dst in ((tok, ln), (sb.at[0], la)):
                if half % 128 == 0:
                    start = pl.multiple_of(k * chunk + core * half, 128)
                    piece = ref[0:rows, pl.ds(start, half)]
                else:
                    both = ref[0:rows, k * chunk : (k + 1) * chunk].astype(F32)
                    piece = jnp.where(core == 0, both[:, :half], both[:, half:]).astype(BF)
                dst[k * half : (k + 1) * half, s * rows : (s + 1) * rows] = piece.T
    for a in range(depth):
        part, off = a * cols // width, a * cols % width
        span = slice(off, off + cols)
        if part < 3:
            left, right0, right1 = ln, s0[1 + part, :, span], s1[1 + part, :, span]
        else:
            left, right0, right1 = la, t0[rows:, span], t1[rows:, span]
        for k in range(chips):
            own = slice(k * half, (k + 1) * half)
            tile = nn(left[own, :rows], right0) + nn(left[own, rows:], right1)
            acc[meta[CHIP] ^ k, meta[ZPOS] ^ a] = tile.astype(BF)
    mid = depth // 2
    copies = []
    top = chips.bit_length() - 2
    for js, dst, zs in (
        (with_bit(chips, 0), ps, slice(0, mid)),
        (without_bit(chips, 0), pk, slice(0, mid)),
        (with_bit(chips, top), qs, slice(mid, depth)),
        (without_bit(chips, top), qk, slice(mid, depth)),
    ):
        for i, j in enumerate(js):
            copies.append(pltpu.make_async_copy(acc.at[j, zs], dst.at[i], sem.at[len(copies)]))
    for copy in copies:
        copy.start()
    for copy in copies:
        copy.wait()


def attention_grads(meta, chips, depth, t0, t1, s0, s1):
    _, rows, width = s0.shape
    half = width // chips // 2
    cols = 4 * width // depth
    piece = struct((chips // 2, depth // 2, half, cols), BF)
    return call(
        partial(attention_grads_kernel, chips, depth),
        meta,
        (t0, t1, s0, s1),
        [whole(t0.shape), whole(t0.shape), whole(s0.shape), whole(s0.shape)],
        (piece,) * 4,
        (ANY,) * 4,
        scratch=[
            pltpu.VMEM((chips * half, 2 * rows), BF),
            pltpu.VMEM((chips * half, 2 * rows), BF),
            pltpu.VMEM((chips, depth, half, cols), BF),
            pltpu.SemaphoreType.DMA((2 * chips,)),
        ],
        flops=2 * 2 * rows * chips * half * 4 * width,
    )


def load_pieces(meta, pieces, wet, ws, sem):
    size = ws.shape[0] // len(pieces)
    copies = []
    for j, piece in enumerate(pieces):
        start = pl.multiple_of((meta[CHIP] ^ j) * size, 16)
        for m, dst in enumerate((wet, ws)):
            copies.append(
                pltpu.make_async_copy(
                    piece.at[pl.ds(m * size, size)], dst.at[pl.ds(start, size)], sem.at[2 * j + m]
                )
            )
    for copy in copies:
        copy.start()
    return copies


def feed_kernel(chips, foreign, meta, *refs):
    toks, refs = refs[:4], refs[4:]
    if foreign:
        pieces, bias_ref, refs = refs[:chips], refs[chips], refs[chips + 1 :]
    else:
        (we, ws, bias_ref), refs = refs[:3], refs[3:]
    act_ref, eg_ref, bias_out, ps, pk, qs, qk = refs[:7]
    x, bg, act_t, eg_t, gx, gs, sem_in, sem_out = refs[7:15]
    rows = toks[0].shape[0] // 2
    width = x.shape[1]
    hidden = act_t.shape[0]
    loads = []
    for r, tok in enumerate(toks):
        for m, dst in enumerate((x, bg)):
            loads.append(
                pltpu.make_async_copy(
                    tok.at[pl.ds(m * rows, rows)],
                    dst.at[pl.ds(r * rows, rows)],
                    sem_in.at[2 * r + m],
                )
            )
    for copy in loads:
        copy.start()
    if foreign:
        we, ws, sem_w = refs[15:18]
        for copy in load_pieces(meta, pieces, we, ws, sem_w):
            copy.wait()
    step = min(256, hidden)
    for r in range(4):
        loads[2 * r].wait()
        loads[2 * r + 1].wait()
        here = slice(r * rows, (r + 1) * rows)
        for h in range(0, hidden, step):
            block = slice(h, h + step)
            if foreign:
                v = nt(x[here, :], we[block, :])
            else:
                v = nn(x[here, :], we[:, block])
            v = v + bias_ref[:, block]
            square = v * v
            t = jnp.tanh(0.7978845608 * v * (1.0 + 0.044715 * square))
            low = 0.5 * (1.0 + t)
            slope = low + 0.5 * v * (1.0 - t * t) * (0.7978845608 * (1.0 + 0.134145 * square))
            act = (v * low).astype(BF)
            eg = (nt(bg[here, :], ws[block, :]) * slope).astype(BF)
            act_ref[here, block] = act
            eg_ref[here, block] = eg
            act_t[block, here] = act.T
            eg_t[block, here] = eg.T
            total = jnp.sum(eg.astype(F32), axis=0, keepdims=True)
            if r == 0:
                bias_out[:, block] = total
            else:
                bias_out[:, block] = bias_out[:, block] + total
    chunk = width // chips
    half = chunk // 2
    core = meta[CORE]
    for k in range(chips):
        span = slice(k * chunk, (k + 1) * chunk)
        for left, right, dst in ((eg_t, x, gx), (act_t, bg, gs)):
            tile = nn(left[...], right[:, span]).astype(BF)
            for a in range(2):
                dst[meta[CHIP] ^ k, core ^ a] = tile[:, a * half : (a + 1) * half]
    top = chips.bit_length() - 2
    copies = []
    for js, src, dst in (
        (with_bit(chips, 0), gx, ps),
        (without_bit(chips, 0), gx, pk),
        (with_bit(chips, top), gs, qs),
        (without_bit(chips, top), gs, qk),
    ):
        for i, j in enumerate(js):
            copies.append(pltpu.make_async_copy(src.at[j], dst.at[i], sem_out.at[len(copies)]))
    for copy in copies:
        copy.start()
    for copy in copies:
        copy.wait()


def feed(meta, chips, toks, weights, bias, foreign):
    rows, width = toks[0].shape[0] // 2, toks[0].shape[1]
    hidden = bias.shape[1] if foreign else bias.shape[1] // 2
    half = width // chips // 2
    if foreign:
        weight_specs = [ANY] * chips
        bias_spec = whole((1, hidden))
    else:
        weight_specs = [
            pl.BlockSpec((width, hidden), lambda i, meta: (0, meta[CORE])),
            pl.BlockSpec((hidden, width), lambda i, meta: (meta[CORE], 0)),
        ]
        bias_spec = pl.BlockSpec((1, hidden), lambda i, meta: (0, meta[CORE]))
    piece = struct((chips // 2, 2, hidden, half), BF)
    scratch = [
        pltpu.VMEM((4 * rows, width), BF),
        pltpu.VMEM((4 * rows, width), BF),
        pltpu.VMEM((hidden, 4 * rows), BF),
        pltpu.VMEM((hidden, 4 * rows), BF),
        pltpu.VMEM((chips, 2, hidden, half), BF),
        pltpu.VMEM((chips, 2, hidden, half), BF),
        pltpu.SemaphoreType.DMA((8,)),
        pltpu.SemaphoreType.DMA((2 * chips,)),
    ]
    if foreign:
        scratch += [
            pltpu.VMEM((hidden, width), BF),
            pltpu.VMEM((hidden, width), BF),
            pltpu.SemaphoreType.DMA((2 * chips,)),
        ]
    return call(
        partial(feed_kernel, chips, foreign),
        meta,
        (*toks, *weights, bias),
        [ANY] * 4 + weight_specs + [bias_spec],
        (struct((4 * rows, hidden), BF),) * 2 + (struct((1, hidden), F32),) + (piece,) * 4,
        (whole((4 * rows, hidden)),) * 2 + (whole((1, hidden)),) + (ANY,) * 4,
        scratch=scratch,
        flops=8 * 4 * rows * width * hidden,
    )


def feed_out_kernel(chips, shards, meta, *refs):
    we, ws, act0, eg0 = refs[:4]
    refs = refs[4:]
    others = []
    for _ in range(shards - 1):
        others.append((refs[0], refs[1], refs[2 : 2 + chips]))
        refs = refs[2 + chips :]
    keep, send = refs[:2]
    refs = refs[2:]
    rows = keep.shape[2]
    copies = []
    for n, (_, _, pieces) in enumerate(others):
        copies += load_pieces(meta, pieces, *refs[3 * n : 3 * n + 3])
    for n, copy in enumerate(copies):
        copy.wait()
    for r in (1, 3, 0, 2):
        here = slice(r * rows, (r + 1) * rows)
        dst = send if r % 2 else keep
        grad = nt(eg0[here, :], we[...])
        for n, (_, eg, _) in enumerate(others):
            grad = grad + nn(eg[here, :], refs[3 * n][...])
        dst[0, r // 2] = grad.astype(BF)
        out = nn(act0[here, :], ws[...])
        for n, (act, _, _) in enumerate(others):
            out = out + nn(act[here, :], refs[3 * n + 1][...])
        dst[1, r // 2] = out.astype(BF)


def feed_out(meta, chips, we, ws, own, others):
    hidden, (width, rows4) = own[0].shape[1], (we.shape[0], own[0].shape[0])
    args = [we, ws, *own]
    specs = [
        pl.BlockSpec((width, hidden), lambda i, meta: (0, meta[CORE])),
        pl.BlockSpec((hidden, width), lambda i, meta: (meta[CORE], 0)),
        whole(own[0].shape),
        whole(own[0].shape),
    ]
    scratch = []
    for act, eg, pieces in others:
        args += [act, eg, *pieces]
        specs += [whole(act.shape), whole(act.shape)] + [ANY] * chips
        scratch += [
            pltpu.VMEM((hidden, width), BF),
            pltpu.VMEM((hidden, width), BF),
            pltpu.SemaphoreType.DMA((2 * chips,)),
        ]
    result = struct((2, 2, rows4 // 4, width), BF)
    return call(
        partial(feed_out_kernel, chips, 1 + len(others)),
        meta,
        tuple(args),
        specs,
        (result, result),
        (whole(result.shape), whole(result.shape)),
        scratch=scratch,
        flops=4 * rows4 * width * hidden * (1 + len(others)),
    )


def norm_back_kernel(meta, x_ref, u_ref, gain_ref, g0, g1, g2, g3, out_ref, gain_out, shift_out):
    rows, width = x_ref.shape
    step = 64
    count = meta[COUNT].astype(F32)
    gain_sum = jnp.zeros((1, width), F32)
    shift_sum = jnp.zeros((1, width), F32)
    for r in range(0, rows, step):
        here = slice(r, r + step)
        xhat, inverse = normalize(x_ref[here, :].astype(F32))
        grad = g0[here, :] + g1[0, 0, here, :].astype(F32) + g2[0, 0, here, :].astype(F32)
        grad = grad + g3[0, here, :].astype(F32)
        gain_sum = gain_sum + jnp.sum(grad * xhat, axis=0, keepdims=True)
        shift_sum = shift_sum + jnp.sum(grad, axis=0, keepdims=True)
        scaled = grad * gain_ref[...]
        mean = jnp.mean(scaled, axis=-1, keepdims=True)
        dot = jnp.mean(scaled * xhat, axis=-1, keepdims=True)
        out_ref[here, :] = u_ref[here, :].astype(F32) * count + inverse * (
            scaled - mean - xhat * dot
        )
    gain_out[...] = gain_sum
    shift_out[...] = shift_sum


def norm_back(meta, x, u, gain, g0, g1, g2, g3):
    rows, width = x.shape
    first = pl.BlockSpec((1, 1, rows, width), lambda i, meta: (0, 0, 0, 0))
    return call(
        norm_back_kernel,
        meta,
        (x, u, gain, g0, g1, g2, g3),
        [
            whole(x.shape),
            whole(x.shape),
            whole((1, width)),
            whole(x.shape),
            first,
            first,
            pl.BlockSpec((1, rows, width), lambda i, meta: (0, 0, 0)),
        ],
        (struct((rows, width), F32), struct((1, width), F32), struct((1, width), F32)),
        (whole(x.shape), whole((1, width)), whole((1, width))),
        vmem=24,
        flops=30 * rows * width,
    )


def exchange(x, axis, flip):
    n = lax.axis_size(axis)
    return lax.ppermute(x, axis, [(i, i ^ flip) for i in range(n)])


def split_bit(x, ascending):
    if ascending:
        return x[0::2], x[1::2]
    middle = x.shape[0] // 2
    return x[:middle], x[middle:]


def reduce_chips(send, keep, bits):
    ascending = len(bits) < 2 or bits[0] < bits[1]
    stays = [keep.astype(F32), exchange(send, "dp", 2 << bits[0]).astype(F32)]
    for bit in bits[1:]:
        halves = [split_bit(s, ascending) for s in stays]
        send = sum(h[1] for h in halves).astype(BF)
        stays = [h[0] for h in halves] + [exchange(send, "dp", 2 << bit).astype(F32)]
    return sum(stays)[0]


def local(
    residual_in,
    upstream,
    layer_norm_gain,
    layer_norm_bias,
    attend_weight,
    output_weight,
    expand_weight,
    expand_bias,
    shrink_weight,
    shrink_bias,
    seq_lengths,
    terminal_pos,
    window_offset,
):
    rows, width = residual_in.shape
    data_ways, depth = lax.axis_size("dp"), lax.axis_size("mp")
    chips = data_ways // 2
    shards = depth // 2
    shard = expand_weight.shape[1]
    hidden = shard // 2
    share = hidden // chips
    half = width // data_ways
    up = list(range(chips.bit_length() - 1))
    down = up[::-1]

    place, zpos = lax.axis_index("dp"), lax.axis_index("mp")
    core, chip = place & 1, place >> 1
    lengths = lax.dynamic_slice_in_dim(seq_lengths[0], zpos * SEQ_DEV, SEQ_DEV)
    head = jnp.stack([core, chip, zpos, jnp.sum(lengths), jnp.sum(seq_lengths[0])])
    meta = jnp.concatenate(
        [head.astype(jnp.int32), lengths, terminal_pos[0], window_offset[0]]
    ).astype(jnp.int32)
    gain = layer_norm_gain[None, :]

    start = core * hidden + chip * share
    bias_half = lax.dynamic_slice_in_dim(expand_bias, core * hidden, hidden)
    high = lax.reduce_precision(bias_half, 8, 7)
    middle = lax.reduce_precision(bias_half - high, 8, 7)
    lowest = bias_half - high - middle
    bias_rows = jnp.pad(
        jnp.stack([high, middle, lowest]).astype(BF), ((0, 13), (0, width - hidden))
    )
    packed = jnp.concatenate(
        [
            lax.dynamic_slice_in_dim(expand_weight, start, share, axis=1).T,
            lax.dynamic_slice_in_dim(shrink_weight, start, share, axis=0),
            bias_rows,
        ]
    )
    shares = [exchange(packed, "mp", 2 * k) for k in range(1, shards)]

    tok, shrink_bias_grad = prepare(meta, residual_in, upstream, gain, layer_norm_bias[None, :])
    tok_core = exchange(tok, "dp", 1)
    tok_deep = exchange(tok, "mp", 1)
    tok_both = exchange(tok_deep, "dp", 1)
    toks = (tok, tok_core, tok_deep, tok_both)

    foreign = []
    for arrived in shares:
        pieces = [arrived] + [exchange(arrived, "dp", 2 * j) for j in range(1, chips)]
        parts = arrived[2 * share : 2 * share + 3, :hidden].astype(F32)
        foreign.append((pieces, (parts[0] + parts[1] + parts[2])[None, :]))

    sides = attention(meta, tok, attend_weight, output_weight)
    sides_core = exchange(sides, "dp", 1)
    attn = attention_grads(meta, chips, depth, tok, tok_core, sides, sides_core)
    attn_low = reduce_chips(attn[0], attn[1], up)
    attn_high = reduce_chips(attn[2], attn[3], down)
    attn_parts = [a[z] for a in (attn_low, attn_high) for z in range(depth // 2)]
    attn_own = attn_parts[0]
    for j in range(1, depth):
        attn_own = attn_own + exchange(attn_parts[j].astype(BF), "mp", j).astype(F32)
    attn_own = attn_own.astype(BF)
    attn_all = [attn_own] + [exchange(attn_own, "mp", j) for j in range(1, depth)]
    grad_attention, attention_out = attention_back(meta, sides, attend_weight, output_weight)

    own = feed(meta, chips, toks, (expand_weight, shrink_weight), expand_bias[None, :], False)
    others = [feed(meta, chips, toks, pieces, bias, True) for pieces, bias in foreign]
    keep, send = feed_out(
        meta,
        chips,
        expand_weight,
        shrink_weight,
        own[:2],
        [(o[0], o[1], pieces) for o, (pieces, _) in zip(others, foreign)],
    )
    passed = exchange(send, "dp", 1)
    crossing = (keep[:, 1].astype(F32) + passed[:, 1].astype(F32)).astype(BF)
    crossed_grad = exchange(crossing[0:1], "mp", 1)
    crossed_out = exchange(crossing[1:2], "mp", 1)

    sums = [
        (reduce_chips(f[3], f[4], up), reduce_chips(f[5], f[6], down)) for f in (*others, own)
    ]
    mlp = list(sums[-1])
    for k, pair in enumerate(sums[:-1]):
        both = exchange(jnp.stack(pair).astype(BF), "mp", 2 * (k + 1)).astype(F32)
        mlp = [mlp[0] + both[0], mlp[1] + both[1]]
    mlp = jnp.stack(mlp)
    mine = mlp[:, 0]
    sibling = exchange(mlp[:, 1].astype(BF), "dp", 1).astype(F32)

    grad_rows, gain_sum, shift_sum = norm_back(
        meta, residual_in, upstream, gain, grad_attention, keep, passed, crossed_grad
    )
    live = (jnp.arange(rows, dtype=jnp.int32) < meta[LIVE])[:, None]
    branch = attention_out + keep[1, 0].astype(F32) + passed[1, 0].astype(F32)
    branch = branch + crossed_out[0].astype(F32) + shrink_bias
    residual_out = (
        residual_in.astype(F32) + jnp.where(live, branch, 0.0)
    ).astype(BF)

    def half_row(v):
        row = jnp.concatenate([jnp.where(core == 0, v, 0.0), jnp.where(core == 1, v, 0.0)], axis=1)
        return jnp.pad(row, ((0, 0), (0, width - shard)))

    count_row = jnp.full((1, width), meta[COUNT].astype(F32))
    small = jnp.concatenate(
        [gain_sum, shift_sum, shrink_bias_grad, count_row, half_row(own[2])]
        + [half_row(o[2]) for o in others]
    )
    for bit in range(depth.bit_length() - 1):
        other = exchange(small, "mp", 1 << bit)
        rest = [small[4 + k] for k in range(shards)]
        if bit > 0:
            step = 1 << (bit - 1)
            rest = [
                r if k & step else r + other[4 + (k | step)] for k, r in enumerate(rest)
            ]
        small = jnp.concatenate([small[:4] + other[:4], jnp.stack(rest)])
    small = small[:5]
    for bit in range(data_ways.bit_length() - 1):
        small = small + exchange(small, "dp", 1 << bit)
    scale = (data_ways * depth) / small[3, 0]

    attn_stack = [a.astype(F32) for a in attn_all]
    parts = []
    for a in range(depth):
        part = attn_stack[0]
        for j in range(1, depth):
            part = jnp.where((zpos ^ a) == j, attn_stack[j], part)
        parts.append(part * scale)
    split = 3 * depth // 4
    attend_sum = jnp.concatenate(parts[:split], axis=1)
    output_sum = jnp.concatenate(parts[split:], axis=1)
    low = jnp.where(core == 0, mine, sibling)
    top = jnp.where(core == 0, sibling, mine)
    mlp_sum = jnp.concatenate([low, top], axis=1) * scale
    return (
        residual_out,
        grad_rows * scale,
        small[0] * scale,
        small[1] * scale,
        attend_sum,
        output_sum,
        mlp_sum[0].T,
        small[4, :shard] * scale,
        mlp_sum[1],
        small[2] * scale,
    )


def solution(mesh):
    in_specs = (
        P(("dp", "mp"), None),
        P(("dp", "mp"), None),
        P(),
        P(),
        P(),
        P(),
        P(None, "mp"),
        P("mp"),
        P("mp", None),
        P(),
        P("dp", None),
        P("dp", "mp"),
        P("dp", "mp"),
    )
    out_specs = (
        P(("dp", "mp"), None),
        P(("dp", "mp"), None),
        P(),
        P(),
        P("dp", None),
        P("dp", None),
        P("dp", "mp"),
        P("mp"),
        P("mp", "dp"),
        P(),
    )
    return jax.shard_map(local, mesh=mesh, in_specs=in_specs, out_specs=out_specs, check_vma=False)
```

```python
from functools import partial

import numpy as np

import jax
import jax.numpy as jnp
from jax import lax
from jax.experimental import pallas as pl
from jax.experimental.pallas import tpu as pltpu
from jax.sharding import PartitionSpec as P

HEADS = 16
HEAD_DIM = 64
ROT = 32
SEQ_DEV = 4
EPSILON = 1e-05
NEGATIVE = -1e30
LANES = 256
BF = jnp.bfloat16
F32 = jnp.float32
MIB = 1 << 20
BIAS_ROWS = 16
US = 0.1
SUMS = 4

COUNT, LIVE, ENDS, STARTS, TERMS, OFFS, TABLE = 0, 1, 2, 6, 10, 14, 24


def nn(a, b):
    return lax.dot_general(a, b, (((1,), (0,)), ((), ())), preferred_element_type=F32)


def nt(a, b):
    return lax.dot_general(a, b, (((1,), (1,)), ((), ())), preferred_element_type=F32)


def call(kernel, args, outs, scratch=(), specs=None, out_specs=None, grid=None, vmem=24, us=US, after=()):
    count = len(args)
    specs = specs or {}

    def body(*refs):
        kernel(*refs[:count], *refs[count + len(after) :])

    single = not isinstance(outs, tuple)
    options = {} if grid is None else {"grid": grid}
    return pl.pallas_call(
        body,
        in_specs=[specs.get(n, VMEM) for n in range(count)] + [ANY] * len(after),
        out_specs=out_specs or (VMEM if single else (VMEM,) * len(outs)),
        out_shape=outs,
        scratch_shapes=list(scratch),
        compiler_params=pltpu.CompilerParams(vmem_limit_bytes=vmem * MIB),
        cost_estimate=pl.CostEstimate(
            flops=int(us * 1e9), bytes_accessed=1024, transcendentals=0
        ),
        **options,
    )(*args, *after)


def places():
    place = lax.axis_index("dp")
    return lax.bitwise_and(place, 1), lax.shift_right_logical(place, 1), lax.axis_index("mp")


VMEM = pl.BlockSpec(memory_space=pltpu.VMEM)
SMEM = pl.BlockSpec(memory_space=pltpu.SMEM)
HBM = pl.BlockSpec(memory_space=pltpu.HBM)
ANY = pl.BlockSpec(memory_space=pl.ANY)


def struct(shape, dtype):
    return jax.ShapeDtypeStruct(shape, dtype)


def normalize(hidden):
    mean = jnp.mean(hidden, axis=-1, keepdims=True)
    removed = hidden - mean
    variance = jnp.mean(removed * removed, axis=-1, keepdims=True)
    inverse = lax.rsqrt(variance + EPSILON)
    return removed * inverse, inverse


def pack_kernel(chips, eb_ref, we_ref, ws_ref, pack_ref, row_ref, sem):
    width = we_ref.shape[0]
    hidden = ws_ref.shape[0] // 2
    share, strip = hidden // chips, width // chips
    core, chip, _ = places()
    half = pl.ds(pl.multiple_of(core * hidden, 128), hidden)
    start = pl.multiple_of(core * hidden + chip * share, 16)
    copies = [
        pltpu.make_async_copy(eb_ref.at[:, half], row_ref, sem.at[0]),
        pltpu.make_async_copy(
            we_ref.at[pl.ds(pl.multiple_of(chip * strip, 16), strip), half],
            pack_ref.at[pl.ds(0, strip), pl.ds(0, hidden)],
            sem.at[1],
        ),
    ]
    for b in range(width // hidden):
        copies.append(
            pltpu.make_async_copy(
                ws_ref.at[pl.ds(start, share), pl.ds(b * hidden, hidden)],
                pack_ref.at[pl.ds(b * share, share), pl.ds(hidden, hidden)],
                sem.at[2 + b],
            )
        )
    for copy in copies:
        copy.start()
    copies[0].wait()
    bias = row_ref[...]
    high = bias.astype(BF)
    middle = (bias - high.astype(F32)).astype(BF)
    lowest = (bias - high.astype(F32) - middle.astype(F32)).astype(BF)
    line = lax.broadcasted_iota(jnp.int32, (BIAS_ROWS, hidden), 0)
    table = jnp.where(line == 0, high.astype(F32), 0.0)
    table = jnp.where(line == 1, middle.astype(F32), table)
    table = jnp.where(line == 2, lowest.astype(F32), table)
    pack_ref[strip:, :hidden] = table.astype(BF)
    pack_ref[strip:, hidden:] = jnp.zeros((BIAS_ROWS, hidden), BF)
    for copy in copies[1:]:
        copy.wait()


def pack(chips, eb, we, ws):
    width, hidden = we.shape[0], ws.shape[0] // 2
    return call(
        partial(pack_kernel, chips),
        (eb, we, ws),
        struct((width // chips + BIAS_ROWS, 2 * hidden), BF),
        scratch=[
            pltpu.VMEM((1, hidden), F32),
            pltpu.SemaphoreType.DMA((2 + width // hidden,)),
        ],
        specs={0: HBM, 1: HBM, 2: HBM},
        vmem=59,
    )


def prepare_kernel(
    lens_ref,
    terms_ref,
    offs_ref,
    x_hbm,
    u_hbm,
    gain_hbm,
    bias_hbm,
    info,
    normed_ref,
    grad_ref,
    sum_ref,
    x_ref,
    u_ref,
    gain_ref,
    bias_ref,
    sem,
):
    rows, width = x_ref.shape
    zpos = places()[2]
    copies = [
        pltpu.make_async_copy(src, dst, sem.at[n])
        for n, (src, dst) in enumerate(
            ((x_hbm, x_ref), (gain_hbm, gain_ref), (bias_hbm, bias_ref), (u_hbm, u_ref))
        )
    ]
    for copy in copies:
        copy.start()

    def note(row, number):
        info[row : row + 1, :] = jnp.zeros((1, info.shape[1]), jnp.int32) + number

    live = 0
    for s in range(SEQ_DEV):
        note(STARTS + s, live)
        live = live + lens_ref[0, zpos * SEQ_DEV + s]
        note(ENDS + s, live)
        note(TERMS + s, terms_ref[0, s])
        note(OFFS + s, offs_ref[0, s])
    total = 0
    for s in range(lens_ref.shape[1]):
        total = total + lens_ref[0, s]
    note(LIVE, live)
    note(COUNT, total)
    step = 64
    count = total.astype(F32)
    sums = jnp.zeros((1, width), F32)
    for copy in copies:
        copy.wait()
    for r in range(0, rows, step):
        xhat, _ = normalize(x_ref[r : r + step, :].astype(F32))
        normed_ref[r : r + step, :] = (xhat * gain_ref[...] + bias_ref[...]).astype(BF)
        where = lax.broadcasted_iota(jnp.int32, (step, width), 0) + r
        grad = jnp.where(where < live, u_ref[r : r + step, :].astype(F32) * count, 0.0).astype(BF)
        grad_ref[r : r + step, :] = grad
        sums = sums + jnp.sum(grad.astype(F32), axis=0, keepdims=True)
    sum_ref[...] = sums


def prepare(lens, terms, offs, x, u, gain, bias, after=()):
    rows, width = x.shape
    return call(
        prepare_kernel,
        (lens, terms, offs, x, u, gain, bias),
        (
            struct((TABLE, LANES), jnp.int32),
            struct((rows, width), BF),
            struct((rows, width), BF),
            struct((1, width), F32),
        ),
        scratch=[
            pltpu.VMEM((rows, width), BF),
            pltpu.VMEM((rows, width), BF),
            pltpu.VMEM((1, width), F32),
            pltpu.VMEM((1, width), F32),
            pltpu.SemaphoreType.DMA((4,)),
        ],
        specs={0: SMEM, 1: SMEM, 2: SMEM, 3: HBM, 4: HBM, 5: HBM, 6: HBM},
        vmem=58,
        after=after,
    )


def slot_of(place, ends):
    index = jnp.zeros(place.shape, jnp.int32)
    for end in ends:
        index = index + (place >= end).astype(jnp.int32)
    return index


def attention_kernel(
    info, normed_ref, bg_ref, freq_ref, wa_hbm, wo_hbm, *refs
):
    out_ref, cos_ref, sin_ref, mask_ref, wa_ref, wo_ref, sem = refs
    rows, lanes = cos_ref.shape
    width = normed_ref.shape[1]
    blocks = width // lanes
    copies = []
    for n in range(blocks):
        here = slice(n * lanes, (n + 1) * lanes)
        for p in range(3):
            cols = slice(p * width + n * lanes, p * width + (n + 1) * lanes)
            copies.append(
                pltpu.make_async_copy(wa_hbm.at[:, cols], wa_ref.at[n, p], sem.at[4 * n + p])
            )
        copies.append(
            pltpu.make_async_copy(wo_hbm.at[here, :], wo_ref.at[here, :], sem.at[4 * n + 3])
        )
    for copy in copies:
        copy.start()

    def tables():
        ends = [info[ENDS + s : ENDS + s + 1, :] for s in range(SEQ_DEV)]
        place = lax.broadcasted_iota(jnp.int32, (rows, lanes), 0)
        index = slot_of(place, ends)
        start = jnp.zeros(place.shape, jnp.int32)
        terminal = jnp.zeros(place.shape, jnp.int32)
        offset = jnp.zeros(place.shape, jnp.int32)
        for s in range(SEQ_DEV):
            here = index == s
            start = jnp.where(here, info[STARTS + s : STARTS + s + 1, :], start)
            terminal = jnp.where(here, info[TERMS + s : TERMS + s + 1, :], terminal)
            offset = jnp.where(here, info[OFFS + s : OFFS + s + 1, :], offset)
        local = place - start
        position = jnp.where(local <= terminal, offset + local, local - terminal - 1)
        angle = position.astype(F32) * freq_ref[...]
        parity = lax.broadcasted_iota(jnp.int32, (rows, lanes), 1) % 2
        sine = jnp.sin(angle)
        cos_ref[...] = jnp.cos(angle)
        sin_ref[...] = jnp.where(parity == 0, -sine, sine)
        key = lax.broadcasted_iota(jnp.int32, (rows, rows), 0)
        query = lax.broadcasted_iota(jnp.int32, (rows, rows), 1)
        allowed = (slot_of(key, ends) == slot_of(query, ends)) & (key <= query)
        mask_ref[...] = jnp.where(allowed, 0.0, NEGATIVE)

    tables()
    even = lax.broadcasted_iota(jnp.int32, (rows, lanes), 1) % 2 == 0

    def swap(v):
        return jnp.where(even, pltpu.roll(v, lanes - 1, 1), pltpu.roll(v, 1, 1))

    def turn(v):
        return v * cos_ref[...] + swap(v) * sin_ref[...]

    def turn_back(v):
        return v * cos_ref[...] - swap(v) * sin_ref[...]

    scale = HEAD_DIM ** (-0.5)
    for n in range(blocks):
        for copy in copies[4 * n : 4 * n + 4]:
            copy.wait()
        here = slice(n * lanes, (n + 1) * lanes)
        attention_heads(
            normed_ref,
            bg_ref,
            wa_ref.at[n],
            wo_ref.at[here],
            mask_ref,
            [out_ref.at[m, :, here] for m in range(4)],
            turn,
            turn_back,
        )


def attention_heads(normed_ref, bg_ref, wa_ref, wo_ref, mask_ref, outs, turn, turn_back):
    rows, lanes = outs[0].shape
    scale = HEAD_DIM ** (-0.5)
    normed = normed_ref[...]
    queries = (turn(nn(normed, wa_ref[0])) * scale).astype(BF)
    keys = turn(nn(normed, wa_ref[1])).astype(BF)
    values = nn(normed, wa_ref[2]).astype(BF)
    grads = nt(bg_ref[...], wo_ref[...]).astype(BF)
    pair = 2 * HEAD_DIM
    lane = lax.broadcasted_iota(jnp.int32, (rows, pair), 1)
    masks = [lane < HEAD_DIM, lane >= HEAD_DIM]

    def one(v, h):
        return jnp.where(masks[h], v, jnp.zeros_like(v))

    queries_t = queries.T
    grads_t = grads.T
    keys_t = keys.T
    values_t = values.T
    attended_t, query_grad_t, key_grads, value_grads = [], [], [], []
    for p in range(lanes // pair):
        cols = slice(p * pair, (p + 1) * pair)
        q2, k2, v2, g2 = queries[:, cols], keys[:, cols], values[:, cols], grads[:, cols]
        scores2 = nn(jnp.concatenate([one(k2, 0), one(k2, 1)], axis=0), queries_t[cols, :])
        pg2 = nn(jnp.concatenate([one(v2, 0), one(v2, 1)], axis=0), grads_t[cols, :])
        key_grad = jnp.zeros((rows, pair), F32)
        value_grad = jnp.zeros((rows, pair), F32)
        for h in range(2):
            head = slice(p * pair + h * HEAD_DIM, p * pair + (h + 1) * HEAD_DIM)
            scores = scores2[h * rows : (h + 1) * rows] + mask_ref[...]
            exponent = jnp.exp(scores - jnp.max(scores, axis=0, keepdims=True))
            probs = exponent * (1.0 / jnp.sum(exponent, axis=0, keepdims=True))
            probs_low = probs.astype(BF)
            probs_grad = pg2[h * rows : (h + 1) * rows]
            row_dot = jnp.sum(probs * probs_grad, axis=0, keepdims=True)
            scores_grad = (probs * (probs_grad - row_dot)).astype(BF)
            attended_t.append(nn(values_t[head, :], probs_low))
            query_grad_t.append(nn(keys_t[head, :], scores_grad))
            key_grad = key_grad + nn(scores_grad, one(q2, h))
            value_grad = value_grad + nn(probs_low, one(g2, h))
        key_grads.append(key_grad)
        value_grads.append(value_grad)
    outs[0][...] = jnp.concatenate(attended_t, axis=0).T.astype(BF)
    outs[1][...] = turn_back(jnp.concatenate(query_grad_t, axis=0).T * scale).astype(BF)
    outs[2][...] = turn_back(jnp.concatenate(key_grads, axis=1)).astype(BF)
    outs[3][...] = jnp.concatenate(value_grads, axis=1).astype(BF)


def attention(info, normed, bg, attend_weight, output_weight, after=()):
    rows, width = normed.shape
    blocks = width // LANES
    pair = np.arange(LANES) % HEAD_DIM // 2
    freq = np.where(pair < ROT // 2, 10000.0 ** (-2.0 * pair / ROT), 0.0)[None].astype(np.float32)
    return call(
        attention_kernel,
        (info, normed, bg, jnp.asarray(freq), attend_weight, output_weight),
        struct((4, rows, width), BF),
        scratch=[
            pltpu.VMEM((rows, LANES), F32),
            pltpu.VMEM((rows, LANES), F32),
            pltpu.VMEM((rows, rows), F32),
            pltpu.VMEM((blocks, 3, width, LANES), BF),
            pltpu.VMEM((width, width), BF),
            pltpu.SemaphoreType.DMA((4 * blocks,)),
        ],
        specs={4: HBM, 5: HBM},
        vmem=52,
        after=after,
    )


def attention_back_kernel(sides, wa_ref, wo_ref, grad_ref, out_ref):
    width = sides.shape[2]
    grad = nt(sides[1], wa_ref[:, :width])
    grad = grad + nt(sides[2], wa_ref[:, width : 2 * width])
    grad_ref[...] = grad + nt(sides[3], wa_ref[:, 2 * width :])
    out_ref[...] = nn(sides[0], wo_ref[...])


def attention_back(sides, attend_weight, output_weight, after=()):
    _, rows, width = sides.shape
    block = pl.BlockSpec((rows, LANES), lambda i: (0, i))
    specs = {
        0: pl.BlockSpec(sides.shape, lambda i: (0, 0, 0)),
        1: pl.BlockSpec((LANES, 3 * width), lambda i: (i, 0)),
        2: pl.BlockSpec((width, LANES), lambda i: (0, i)),
    }
    return call(
        attention_back_kernel,
        (sides, attend_weight, output_weight),
        (struct((rows, width), F32), struct((rows, width), F32)),
        specs=specs,
        out_specs=(block, block),
        grid=(width // LANES,),
        after=after,
    )


def with_bit(n, bit):
    return [j for j in range(n) if j >> bit & 1]


def without_bit(n, bit):
    return [j for j in range(n) if not j >> bit & 1]


def attention_grads_kernel(
    chips, depth, n0, n1, g0, g1, s0, s1, ps, pk, qs, qk, ln, la, acc, sem
):
    rows, width = n0.shape
    chunk = width // chips
    half = chunk // 2
    cols = 4 * width // depth
    core, chip, zpos = places()
    for s, (tok, sb) in enumerate(((n0, s0), (n1, s1))):
        for k in range(chips):
            for ref, dst in ((tok, ln), (sb.at[0], la)):
                if half % 128 == 0:
                    start = pl.multiple_of(k * chunk + core * half, 128)
                    piece = ref[0:rows, pl.ds(start, half)]
                else:
                    both = ref[0:rows, k * chunk : (k + 1) * chunk].astype(F32)
                    piece = jnp.where(core == 0, both[:, :half], both[:, half:]).astype(BF)
                dst[k * half : (k + 1) * half, s * rows : (s + 1) * rows] = piece.T
    for a in range(depth):
        part, off = a * cols // width, a * cols % width
        span = slice(off, off + cols)
        if part < 3:
            left, right0, right1 = ln, s0[1 + part, :, span], s1[1 + part, :, span]
        else:
            left, right0, right1 = la, g0[:, span], g1[:, span]
        tile = (nn(left[:, :rows], right0) + nn(left[:, rows:], right1)).astype(BF)
        for k in range(chips):
            acc[chip ^ k, zpos ^ a] = tile[k * half : (k + 1) * half]
    mid = depth // 2
    copies = []
    top = chips.bit_length() - 2
    for js, dst, zs in (
        (with_bit(chips, 0), ps, slice(0, mid)),
        (without_bit(chips, 0), pk, slice(0, mid)),
        (with_bit(chips, top), qs, slice(mid, depth)),
        (without_bit(chips, top), qk, slice(mid, depth)),
    ):
        for i, j in enumerate(js):
            copies.append(pltpu.make_async_copy(acc.at[j, zs], dst.at[i], sem.at[len(copies)]))
    for copy in copies:
        copy.start()
    for copy in copies:
        copy.wait()


def attention_grads(chips, depth, own, core, s0, s1, after=()):
    rows, width = own[0].shape
    half = width // chips // 2
    cols = 4 * width // depth
    piece = struct((chips // 2, depth // 2, half, cols), BF)
    return call(
        partial(attention_grads_kernel, chips, depth),
        (own[0], core[0], own[1], core[1], s0, s1),
        (piece,) * 4,
        scratch=[
            pltpu.VMEM((chips * half, 2 * rows), BF),
            pltpu.VMEM((chips * half, 2 * rows), BF),
            pltpu.VMEM((chips, depth, half, cols), BF),
            pltpu.SemaphoreType.DMA((2 * chips,)),
        ],
        after=after,
    )


def load_weights(sources, we, ws, sem):
    hidden, width = ws.shape
    core, place, _ = places()
    if len(sources) == 2:
        half = pl.ds(pl.multiple_of(core * hidden, 128), hidden)
        return [
            pltpu.make_async_copy(sources[0].at[:, half], we, sem.at[0]),
            pltpu.make_async_copy(sources[1].at[half], ws, sem.at[1]),
        ]
    share, strip = hidden // len(sources), width // len(sources)
    copies = []
    for j, piece in enumerate(sources):
        chip = place ^ j
        copies.append(
            pltpu.make_async_copy(
                piece.at[pl.ds(0, strip), pl.ds(0, hidden)],
                we.at[pl.ds(pl.multiple_of(chip * strip, 16), strip)],
                sem.at[len(copies)],
            )
        )
        for b in range(width // hidden):
            copies.append(
                pltpu.make_async_copy(
                    piece.at[pl.ds(b * share, share), pl.ds(hidden, hidden)],
                    ws.at[
                        pl.ds(pl.multiple_of(chip * share, 16), share),
                        pl.ds(b * hidden, hidden),
                    ],
                    sem.at[len(copies)],
                )
            )
    return copies


def weight_scratch(chips, hidden, width):
    return [
        pltpu.VMEM((width, hidden), BF),
        pltpu.VMEM((hidden, width), BF),
        pltpu.SemaphoreType.DMA((chips * (1 + width // hidden),)),
    ]


def feed_kernel(chips, foreign, *refs):
    toks, refs = refs[:8], refs[8:]
    sources = refs[: chips if foreign else 2]
    refs = refs[len(sources) :]
    if not foreign:
        bias_ref, refs = refs[0], refs[1:]
    act_ref, eg_ref, bias_out, ps, pk, qs, qk = refs[:7]
    x, bg, act_t, eg_t, sem_in, we, ws, sem_w = refs[7:15]
    rows, width = toks[0].shape
    hidden = act_t.shape[0]
    weights = load_weights(sources, we, ws, sem_w)
    if foreign:
        bias_rows, sem_b = refs[15:17]
        strip = width // chips
        weights.append(
            pltpu.make_async_copy(sources[0].at[pl.ds(strip, BIAS_ROWS)], bias_rows, sem_b)
        )
    for copy in weights:
        copy.start()
    loads = []
    for n, tok in enumerate(toks):
        dst = (x, bg)[n % 2].at[pl.ds(n // 2 * rows, rows)]
        loads.append(pltpu.make_async_copy(tok, dst, sem_in.at[n]))
    for copy in loads:
        copy.start()
    for copy in weights:
        copy.wait()
    if foreign:
        bias = jnp.sum(bias_rows[:, :hidden].astype(F32), axis=0, keepdims=True)
    else:
        bias = bias_ref[:, pl.ds(pl.multiple_of(places()[0] * hidden, 128), hidden)]
    for copy in loads:
        copy.wait()
    step = min(256, hidden)
    for h in range(0, hidden, step):
        block = slice(h, h + step)
        v = nn(x[...], we[:, block]) + bias[:, block]
        square = v * v
        t = jnp.tanh(0.7978845608 * v * (1.0 + 0.044715 * square))
        low = 0.5 * (1.0 + t)
        slope = low + 0.5 * v * (1.0 - t * t) * (0.7978845608 * (1.0 + 0.134145 * square))
        act = (v * low).astype(BF)
        eg = (nt(bg[...], ws[block, :]) * slope).astype(BF)
        act_ref[:, block] = act
        eg_ref[:, block] = eg
        act_t[block, :] = act.T
        eg_t[block, :] = eg.T
        bias_out[:, block] = jnp.sum(eg.astype(F32), axis=0, keepdims=True)
    chunk = width // chips
    half = chunk // 2
    core, chip, _ = places()
    top = chips.bit_length() - 2
    for left, right, bit, send, keep in ((eg_t, x, 0, ps, pk), (act_t, bg, top, qs, qk)):
        for dst, js in ((send, with_bit(chips, bit)), (keep, without_bit(chips, bit))):
            for i, j in enumerate(js):
                if half % 128 == 0:
                    start = pl.multiple_of((chip ^ j) * chunk, 128)
                    tile = nn(left[...], right[:, pl.ds(start, chunk)]).astype(BF)
                    for a in range(2):
                        dst[i, core ^ a] = tile[:, a * half : (a + 1) * half]
                    continue
                for k in range(chips):

                    @pl.when(chip ^ j == k)
                    def narrow():
                        tile = nn(left[...], right[:, k * chunk : (k + 1) * chunk]).astype(BF)
                        for a in range(2):
                            dst[i, core ^ a] = tile[:, a * half : (a + 1) * half].T


def feed(chips, toks, weights, bias, hidden, after=()):
    rows, width = toks[0].shape
    half = width // chips // 2
    foreign = bias is None
    edge = (hidden, half) if half % 128 == 0 else (half, hidden)
    piece = struct((chips // 2, 2, *edge), BF)
    scratch = [
        pltpu.VMEM((4 * rows, width), BF),
        pltpu.VMEM((4 * rows, width), BF),
        pltpu.VMEM((hidden, 4 * rows), BF),
        pltpu.VMEM((hidden, 4 * rows), BF),
        pltpu.SemaphoreType.DMA((8,)),
        *weight_scratch(chips, hidden, width),
    ]
    args = (*toks, *weights)
    specs = {n: ANY for n in range(len(args))}
    if foreign:
        scratch += [pltpu.VMEM((BIAS_ROWS, 2 * hidden), BF), pltpu.SemaphoreType.DMA(())]
    else:
        args += (bias,)
    return call(
        partial(feed_kernel, chips, foreign),
        args,
        (struct((4 * rows, hidden), BF),) * 2 + (struct((1, hidden), F32),) + (piece,) * 4,
        scratch=scratch,
        specs=specs,
        us=20.0 if foreign else US,
        after=after,
    )


def feed_out_kernel(chips, shards, *refs):
    sets = []
    for n in range(shards):
        size = chips if n else 2
        sets.append((refs[0], refs[1], refs[2 : 2 + size]))
        refs = refs[2 + size :]
    keep, send = refs[:2]
    rows = keep.shape[2]
    scratch = [refs[2 + 3 * n : 5 + 3 * n] for n in range(shards)]
    copies = []
    for (_, _, sources), (we, ws, sem) in zip(sets, scratch):
        copies += load_weights(sources, we, ws, sem)
    for copy in copies:
        copy.start()
    for copy in copies:
        copy.wait()
    width = keep.shape[3]
    step = min(256, width)
    for c in range(0, width, step):
        block = slice(c, c + step)
        grad, out = 0.0, 0.0
        for (act, eg, _), (we, ws, _) in zip(sets, scratch):
            grad = grad + nt(eg[...], we[block, :])
            out = out + nn(act[...], ws[:, block])
        for m, value in enumerate((grad, out)):
            for r in range(4):
                dst = send if r % 2 else keep
                dst[m, r // 2, :, block] = value[r * rows : (r + 1) * rows].astype(BF)


def feed_out(chips, sets, after=()):
    rows4, hidden = sets[0][0].shape
    width = sets[0][2][1].shape[1]
    args, specs, scratch = (), {}, []
    for act, eg, sources in sets:
        for n in range(len(sources)):
            specs[len(args) + 2 + n] = ANY
        args += (act, eg, *sources)
        scratch += weight_scratch(chips, hidden, width)
    result = struct((2, 2, rows4 // 4, width), BF)
    return call(
        partial(feed_out_kernel, chips, len(sets)),
        args,
        (result, result),
        scratch=scratch,
        specs=specs,
        after=after,
    )


def norm_back_kernel(info, x_ref, u_ref, gain_ref, g0, g1, g2, g3, sum_ref, *refs):
    biases, (out_ref, small_ref) = refs[:-2], refs[-2:]
    rows, width = x_ref.shape
    step = 64
    count = info[COUNT : COUNT + 1, 0:1].astype(F32)
    gain_sum = jnp.zeros((1, width), F32)
    shift_sum = jnp.zeros((1, width), F32)
    for r in range(0, rows, step):
        here = slice(r, r + step)
        xhat, inverse = normalize(x_ref[here, :].astype(F32))
        grad = g0[here, :] + g1[0, 0, here, :].astype(F32) + g2[0, 0, here, :].astype(F32)
        grad = grad + g3[0, here, :].astype(F32)
        gain_sum = gain_sum + jnp.sum(grad * xhat, axis=0, keepdims=True)
        shift_sum = shift_sum + jnp.sum(grad, axis=0, keepdims=True)
        scaled = grad * gain_ref[...]
        mean = jnp.mean(scaled, axis=-1, keepdims=True)
        dot = jnp.mean(scaled * xhat, axis=-1, keepdims=True)
        out_ref[here, :] = u_ref[here, :].astype(F32) * count + inverse * (
            scaled - mean - xhat * dot
        )
    small_ref[...] = jnp.zeros(small_ref.shape, F32)
    small_ref[0:1, :] = gain_sum
    small_ref[1:2, :] = shift_sum
    small_ref[2:3, :] = sum_ref[...]
    small_ref[3:4, :] = jnp.zeros((1, width), F32) + count
    hidden = biases[0].shape[1]
    half = pl.ds(pl.multiple_of(places()[0] * hidden, 128), hidden)
    for k, bias in enumerate(biases):
        small_ref[SUMS + k : SUMS + k + 1, half] = bias[...]


def norm_back(info, x, u, gain, g0, g1, g2, g3, sums, biases, after=()):
    small = (SUMS + len(biases), x.shape[1])
    return call(
        norm_back_kernel,
        (info, x, u, gain, g0, g1, g2, g3, sums, *biases),
        (struct(x.shape, F32), struct(small, F32)),
        after=after,
    )


def small_kernel(axis, bit, mine, other, out):
    if axis == "dp":
        out[...] = mine[...] + other[...]
        return
    out[:SUMS, :] = mine[:SUMS, :] + other[:SUMS, :]
    step = (1 << bit) // 2
    for k in range(mine.shape[0] - SUMS):
        row = slice(SUMS + k, SUMS + k + 1)
        if step and not k & step:
            twin = SUMS + (k | step)
            out[row, :] = mine[row, :] + other[twin : twin + 1, :]
        else:
            out[row, :] = mine[row, :]


def small_sum(small, axis, bit):
    other = exchange(small, axis, 1 << bit)
    return call(partial(small_kernel, axis, bit), (small, other), struct(small.shape, F32))


def row_out_kernel(info, x_ref, sum_ref, g1, g2, g3, bias_ref, out_ref):
    rows, width = x_ref.shape
    step = 64
    for r in range(0, rows, step):
        here = slice(r, r + step)
        branch = sum_ref[here, :] + g1[1, 0, here, :].astype(F32) + g2[1, 0, here, :].astype(F32)
        branch = branch + g3[0, here, :].astype(F32) + bias_ref[...]
        where = lax.broadcasted_iota(jnp.int32, (step, width), 0) + r
        branch = jnp.where(where < info[LIVE : LIVE + 1, 0:1], branch, 0.0)
        out_ref[here, :] = (x_ref[here, :].astype(F32) + branch).astype(BF)


def row_out(info, x, attention_out, g1, g2, g3, bias, after=()):
    return call(
        row_out_kernel,
        (info, x, attention_out, g1, g2, g3, bias),
        struct(x.shape, BF),
        after=after,
    )


def attend_final_kernel(scale, small_ref, *refs):
    parts, (attend, output) = refs[:-2], refs[-2:]
    depth = len(parts)
    cols = parts[0].shape[2]
    edge = 3 * depth // 4
    factor = scale / small_ref[3:4, 0:1]
    for j, part in enumerate(parts):
        place = places()[2] ^ j
        value = part[0].astype(F32) * factor

        @pl.when(place < edge)
        def inner():
            attend[:, pl.ds(pl.multiple_of(place * cols, 128), cols)] = value

        @pl.when(place >= edge)
        def outer():
            output[:, pl.ds(pl.multiple_of((place - edge) * cols, 128), cols)] = value


def attend_final(scale, small, parts):
    _, half, cols = parts[0].shape
    depth = len(parts)
    attend, output = (half, 3 * depth // 4 * cols), (half, depth // 4 * cols)
    return call(
        partial(attend_final_kernel, scale),
        (small, *parts),
        (struct(attend, F32), struct(output, F32)),
    )


def row_final_kernel(scale, small_ref, grad_ref, out_ref, gain, shift, bias, expand):
    factor = scale / small_ref[3:4, 0:1]
    out_ref[...] = grad_ref[...] * factor
    gain[...] = small_ref[0:1, :] * factor
    shift[...] = small_ref[1:2, :] * factor
    bias[...] = small_ref[2:3, :] * factor
    expand[...] = small_ref[SUMS : SUMS + 1, : expand.shape[1]] * factor


def row_final(scale, small, grad, shard):
    row = struct((1, grad.shape[1]), F32)
    return call(
        partial(row_final_kernel, scale),
        (small, grad),
        (struct(grad.shape, F32), row, row, row, struct((1, shard), F32)),
    )


def feed_final_kernel(scale, narrow, small_ref, mine, sibling, expand, shrink):
    hidden = mine.shape[2 if narrow else 1]
    factor = scale / small_ref[3:4, 0:1]
    for n, part in enumerate((mine, sibling)):
        start = pl.multiple_of((places()[0] ^ n) * hidden, 128)
        first, second = part[0].astype(F32), part[1].astype(F32)
        expand[:, pl.ds(start, hidden)] = (first if narrow else first.T) * factor
        shrink[pl.ds(start, hidden), :] = (second.T if narrow else second) * factor


def feed_final(scale, small, mine, sibling, half):
    narrow = half % 128 != 0
    hidden = mine.shape[2 if narrow else 1]
    return call(
        partial(feed_final_kernel, scale, narrow),
        (small, mine, sibling),
        (struct((half, 2 * hidden), F32), struct((2 * hidden, half), F32)),
    )


def add_kernel(plan, *refs):
    ins = refs[: len(refs) - len(plan)]
    for out, (_, parts) in zip(refs[len(ins) :], plan):
        for p, part in enumerate(parts):
            out[p] = sum(ins[n][index].astype(F32) for n, index in part).astype(out.dtype)


def add(plan, after=()):
    arrays, outs, inner = [], [], []
    for dtype, parts in plan:
        entries = []
        for part in parts:
            entry = []
            for array, index in part:
                n = next((n for n, a in enumerate(arrays) if a is array), len(arrays))
                if n == len(arrays):
                    arrays.append(array)
                entry.append((n, index))
            entries.append(entry)
        inner.append((dtype, entries))
        array, index = parts[0][0]
        outs.append(struct((len(parts), *array.shape[len(index) :]), dtype))
    return call(partial(add_kernel, inner), tuple(arrays), tuple(outs), after=after)


def exchange(x, axis, flip):
    n = lax.axis_size(axis)
    return lax.ppermute(x, axis, [(i, i ^ flip) for i in range(n)])


def reduce_chips(chips, low, high, afters):
    bits = list(range(chips.bit_length() - 1))
    orders = (bits, bits[::-1])
    left = []
    for (send, keep), order in zip((low, high), orders):
        got = exchange(send, "dp", 2 << order[0])
        left.append([[(keep, (i,)), (got, (i,))] for i in range(chips // 2)])
    sends = ()
    for n in range(1, len(bits)):
        stay, go = [], []
        for entries, order in zip(left, orders):
            if order[0] == 0:
                stay.append(entries[0::2])
                go.append(entries[1::2])
            else:
                stay.append(entries[: len(entries) // 2])
                go.append(entries[len(entries) // 2 :])
        sends = add([(BF, g) for g in go], after=afters)
        left = []
        for entries, send, order in zip(stay, sends, orders):
            got = exchange(send, "dp", 2 << order[n])
            left.append([e + [(got, (i,))] for i, e in enumerate(entries)])
    return (left[0][0], left[1][0]), sends


def behind(x, *others):
    return lax.optimization_barrier((x, *others))[0]


def at(entry, *index):
    return [(array, first + index) for array, first in entry]


def local(
    residual_in,
    upstream,
    layer_norm_gain,
    layer_norm_bias,
    attend_weight,
    output_weight,
    expand_weight,
    expand_bias,
    shrink_weight,
    shrink_bias,
    seq_lengths,
    terminal_pos,
    window_offset,
):
    rows, width = residual_in.shape
    data_ways, depth = lax.axis_size("dp"), lax.axis_size("mp")
    chips = data_ways // 2
    shards = depth // 2
    shard = expand_weight.shape[1]
    hidden = shard // 2
    gain = layer_norm_gain[None, :]
    packed = pack(chips, expand_bias[None, :], expand_weight, shrink_weight)
    shares = [exchange(packed, "mp", 2 * k) for k in range(1, shards)]
    info, normed, bg, shrink_bias_grad = prepare(
        seq_lengths,
        terminal_pos,
        window_offset,
        residual_in,
        upstream,
        gain,
        layer_norm_bias[None, :],
        after=(packed,),
    )
    tok = (normed, bg)
    tok_core = [exchange(t, "dp", 1) for t in tok]

    sides = attention(info, normed, bg, attend_weight, output_weight)
    grad_attention, attention_out = attention_back(sides, attend_weight, output_weight)
    deep_normed = exchange(normed, "mp", 1)
    sides_core = exchange(
        behind(sides, grad_attention, *shares, *tok_core, deep_normed), "dp", 1
    )
    tok_deep = [deep_normed, exchange(behind(bg, sides), "mp", 1)]
    foreign = [[s] + [exchange(s, "dp", 2 * j) for j in range(1, chips)] for s in shares]
    attn = attention_grads(chips, depth, tok, tok_core, sides, sides_core, after=shares)
    tok_both = [exchange(behind(t, attn[0]), "dp", 1) for t in tok_deep]
    attn = [behind(a, *tok_both) for a in attn]
    toks = (*tok, *tok_core, *tok_deep, *tok_both)

    weights = (expand_weight, shrink_weight)
    own = feed(chips, toks, weights, expand_bias[None, :], hidden, after=attn[:1])
    others = [feed(chips, toks, pieces, None, hidden, after=own[:1]) for pieces in foreign]
    sets = [(own[0], own[1], weights)]
    sets += [(o[0], o[1], pieces) for o, pieces in zip(others, foreign)]
    attn_sums, sent = reduce_chips(chips, attn[:2], attn[2:], (others[-1][2],))
    keep, send = feed_out(chips, sets, after=sent)
    passed = exchange(send, "dp", 1)
    crossing = add([(BF, [[(keep, (m, 1)), (passed, (m, 1))]]) for m in range(2)])
    crossed_grad, crossed_out = (exchange(c, "mp", 1) for c in crossing)

    middle = depth // 2
    entries = [at(attn_sums[z // middle], z % middle) for z in range(depth)]
    parts = add([(BF, [e]) for e in entries[1:]])
    arrived = [(exchange(p, "mp", j + 1), (0,)) for j, p in enumerate(parts)]
    attn_own = add([(BF, [entries[0] + arrived])])[0]
    attn_all = [attn_own] + [exchange(attn_own, "mp", j) for j in range(1, depth)]

    mine, away = [[], []], [[], []]
    for k, f in enumerate((*others, own)):
        pair, _ = reduce_chips(chips, f[3:5], f[5:7], (keep,))
        if k < len(others):
            both = add([(BF, [at(p, a) for p in pair for a in range(2)])])[0]
            both = exchange(both, "mp", 2 * (k + 1))
            pair = [[(both, (2 * n,))] for n in range(2)], [[(both, (2 * n + 1,))] for n in range(2)]
        else:
            pair = [at(p, 0) for p in pair], [at(p, 1) for p in pair]
        for n in range(2):
            mine[n] = mine[n] + pair[0][n]
            away[n] = away[n] + pair[1][n]
    mine, away = add([(F32, mine), (BF, away)])
    sibling = exchange(away, "dp", 1)

    grad_rows, small = norm_back(
        info,
        residual_in,
        upstream,
        gain,
        grad_attention,
        keep,
        passed,
        crossed_grad,
        shrink_bias_grad,
        [f[2] for f in (own, *others)],
    )
    residual_out = row_out(
        info, residual_in, attention_out, keep, passed, crossed_out, shrink_bias[None, :]
    )
    for bit in range(depth.bit_length() - 1):
        small = small_sum(small, "mp", bit)
    for bit in range(data_ways.bit_length() - 1):
        small = small_sum(small, "dp", bit)

    factor = float(data_ways * depth)
    attend_sum, output_sum = attend_final(factor, small, attn_all)
    expand_sum, shrink_sum = feed_final(factor, small, mine, sibling, width // data_ways)
    grad_rows, gain_sum, shift_sum, bias_sum, expand_bias_sum = row_final(
        factor, small, grad_rows, shard
    )
    return (
        residual_out,
        grad_rows,
        gain_sum[0],
        shift_sum[0],
        attend_sum,
        output_sum,
        expand_sum,
        expand_bias_sum[0],
        shrink_sum,
        bias_sum[0],
    )


def solution(mesh):
    in_specs = (
        P(("dp", "mp"), None),
        P(("dp", "mp"), None),
        P(),
        P(),
        P(),
        P(),
        P(None, "mp"),
        P("mp"),
        P("mp", None),
        P(),
        P("dp", None),
        P("dp", "mp"),
        P("dp", "mp"),
    )
    out_specs = (
        P(("dp", "mp"), None),
        P(("dp", "mp"), None),
        P(),
        P(),
        P("dp", None),
        P("dp", None),
        P("dp", "mp"),
        P("mp"),
        P("mp", "dp"),
        P(),
    )
    return jax.shard_map(local, mesh=mesh, in_specs=in_specs, out_specs=out_specs, check_vma=False)
```

```python
from functools import partial

import numpy as np

import jax
import jax.numpy as jnp
from jax import lax
from jax.experimental import pallas as pl
from jax.experimental.pallas import tpu as pltpu
from jax.sharding import PartitionSpec as P

HEADS = 16
HEAD_DIM = 64
ROT = 32
SEQ_DEV = 4
EPSILON = 1e-05
NEGATIVE = -1e30
LANES = 256
BF = jnp.bfloat16
F32 = jnp.float32
MIB = 1 << 20
BIAS_ROWS = 16
COST = {'pack': 3, 'prep': 1, 'A': 0.05, 'B': 1, 'A3': 25, 'M': 50, 'cross': 0.3, 'at1': 12, 'fo1': 0.05, 'both': 6, 'parts': 0.05, 'aown': 0.05, 'mine': 3, 'nb': 1, 'ro': 12, 'sm': 50, 'af': 50, 'rf': 25, 'ff': 1, 'zadd': 6, 'zjoin': 1}
CFG = {'deep0': 1, 'deep1': 4, 'sidesB': 1, 'sidesS': 1, 'sidesC': 1, 'sidesD': 0, 'W2': 1, 'A3S': 2, 'bothA3': 1, 'attnBoth': 1, 'MA3': 1, 'cross2': 1, 'at1': 1, 'fo1': 3, 'first': 0, 'nb': 1, 'parts': 0, 'both': 1, 'send': 1}
SUMS = 4

COUNT, LIVE, ENDS, STARTS, TERMS, OFFS, TABLE = 0, 1, 2, 6, 10, 14, 24


def nn(a, b):
    return lax.dot_general(a, b, (((1,), (0,)), ((), ())), preferred_element_type=F32)


def nt(a, b):
    return lax.dot_general(a, b, (((1,), (1,)), ((), ())), preferred_element_type=F32)


def call(kernel, args, outs, scratch=(), specs=None, out_specs=None, grid=None, vmem=24, tag="", after=()):
    count = len(args)
    specs = specs or {}

    def body(*refs):
        kernel(*refs[:count], *refs[count + len(after) :])

    single = not isinstance(outs, tuple)
    options = {} if grid is None else {"grid": grid}
    return pl.pallas_call(
        body,
        in_specs=[specs.get(n, VMEM) for n in range(count)] + [ANY] * len(after),
        out_specs=out_specs or (VMEM if single else (VMEM,) * len(outs)),
        out_shape=outs,
        scratch_shapes=list(scratch),
        compiler_params=pltpu.CompilerParams(vmem_limit_bytes=vmem * MIB),
        cost_estimate=pl.CostEstimate(
            flops=int(COST[tag] * 1e9), bytes_accessed=1024, transcendentals=0
        ),
        **options,
    )(*args, *after)


def places():
    place = lax.axis_index("dp")
    return lax.bitwise_and(place, 1), lax.shift_right_logical(place, 1), lax.axis_index("mp")


VMEM = pl.BlockSpec(memory_space=pltpu.VMEM)
SMEM = pl.BlockSpec(memory_space=pltpu.SMEM)
HBM = pl.BlockSpec(memory_space=pltpu.HBM)
ANY = pl.BlockSpec(memory_space=pl.ANY)


def struct(shape, dtype):
    return jax.ShapeDtypeStruct(shape, dtype)


def normalize(hidden):
    mean = jnp.mean(hidden, axis=-1, keepdims=True)
    removed = hidden - mean
    variance = jnp.mean(removed * removed, axis=-1, keepdims=True)
    inverse = lax.rsqrt(variance + EPSILON)
    return removed * inverse, inverse


def pack_kernel(chips, eb_ref, we_ref, ws_ref, pack_ref, row_ref, sem):
    width = we_ref.shape[0]
    hidden = ws_ref.shape[0] // 2
    share, strip = hidden // chips, width // chips
    core, chip, _ = places()
    half = pl.ds(pl.multiple_of(core * hidden, 128), hidden)
    start = pl.multiple_of(core * hidden + chip * share, 16)
    copies = [
        pltpu.make_async_copy(eb_ref.at[:, half], row_ref, sem.at[0]),
        pltpu.make_async_copy(
            we_ref.at[pl.ds(pl.multiple_of(chip * strip, 16), strip), half],
            pack_ref.at[pl.ds(0, strip), pl.ds(0, hidden)],
            sem.at[1],
        ),
    ]
    for b in range(width // hidden):
        copies.append(
            pltpu.make_async_copy(
                ws_ref.at[pl.ds(start, share), pl.ds(b * hidden, hidden)],
                pack_ref.at[pl.ds(b * share, share), pl.ds(hidden, hidden)],
                sem.at[2 + b],
            )
        )
    for copy in copies:
        copy.start()
    copies[0].wait()
    bias = row_ref[...]
    high = bias.astype(BF)
    middle = (bias - high.astype(F32)).astype(BF)
    lowest = (bias - high.astype(F32) - middle.astype(F32)).astype(BF)
    line = lax.broadcasted_iota(jnp.int32, (BIAS_ROWS, hidden), 0)
    table = jnp.where(line == 0, high.astype(F32), 0.0)
    table = jnp.where(line == 1, middle.astype(F32), table)
    table = jnp.where(line == 2, lowest.astype(F32), table)
    pack_ref[strip:, :hidden] = table.astype(BF)
    pack_ref[strip:, hidden:] = jnp.zeros((BIAS_ROWS, hidden), BF)
    for copy in copies[1:]:
        copy.wait()


def pack(chips, eb, we, ws):
    width, hidden = we.shape[0], ws.shape[0] // 2
    return call(
        partial(pack_kernel, chips),
        (eb, we, ws),
        struct((width // chips + BIAS_ROWS, 2 * hidden), BF),
        scratch=[
            pltpu.VMEM((1, hidden), F32),
            pltpu.SemaphoreType.DMA((2 + width // hidden,)),
        ],
        specs={0: HBM, 1: HBM, 2: HBM},
        vmem=59,
        tag="pack",
    )


def prepare_kernel(
    lens_ref,
    terms_ref,
    offs_ref,
    x_hbm,
    u_hbm,
    gain_hbm,
    bias_hbm,
    info,
    normed_ref,
    grad_ref,
    sum_ref,
    x_ref,
    u_ref,
    gain_ref,
    bias_ref,
    sem,
):
    rows, width = x_ref.shape
    zpos = places()[2]
    copies = [
        pltpu.make_async_copy(src, dst, sem.at[n])
        for n, (src, dst) in enumerate(
            ((x_hbm, x_ref), (gain_hbm, gain_ref), (bias_hbm, bias_ref), (u_hbm, u_ref))
        )
    ]
    for copy in copies:
        copy.start()

    def note(row, number):
        info[row : row + 1, :] = jnp.zeros((1, info.shape[1]), jnp.int32) + number

    live = 0
    for s in range(SEQ_DEV):
        note(STARTS + s, live)
        live = live + lens_ref[0, zpos * SEQ_DEV + s]
        note(ENDS + s, live)
        note(TERMS + s, terms_ref[0, s])
        note(OFFS + s, offs_ref[0, s])
    total = 0
    for s in range(lens_ref.shape[1]):
        total = total + lens_ref[0, s]
    note(LIVE, live)
    note(COUNT, total)
    step = 64
    count = total.astype(F32)
    sums = jnp.zeros((1, width), F32)
    for copy in copies:
        copy.wait()
    for r in range(0, rows, step):
        xhat, _ = normalize(x_ref[r : r + step, :].astype(F32))
        normed_ref[r : r + step, :] = (xhat * gain_ref[...] + bias_ref[...]).astype(BF)
        where = lax.broadcasted_iota(jnp.int32, (step, width), 0) + r
        grad = jnp.where(where < live, u_ref[r : r + step, :].astype(F32) * count, 0.0).astype(BF)
        grad_ref[r : r + step, :] = grad
        sums = sums + jnp.sum(grad.astype(F32), axis=0, keepdims=True)
    sum_ref[...] = sums


def prepare(lens, terms, offs, x, u, gain, bias, after=()):
    rows, width = x.shape
    return call(
        prepare_kernel,
        (lens, terms, offs, x, u, gain, bias),
        (
            struct((TABLE, LANES), jnp.int32),
            struct((rows, width), BF),
            struct((rows, width), BF),
            struct((1, width), F32),
        ),
        scratch=[
            pltpu.VMEM((rows, width), BF),
            pltpu.VMEM((rows, width), BF),
            pltpu.VMEM((1, width), F32),
            pltpu.VMEM((1, width), F32),
            pltpu.SemaphoreType.DMA((4,)),
        ],
        specs={0: SMEM, 1: SMEM, 2: SMEM, 3: HBM, 4: HBM, 5: HBM, 6: HBM},
        vmem=58,
        after=after,
        tag="prep",
    )


def slot_of(place, ends):
    index = jnp.zeros(place.shape, jnp.int32)
    for end in ends:
        index = index + (place >= end).astype(jnp.int32)
    return index


def attention_kernel(
    info, normed_ref, bg_ref, freq_ref, wa_hbm, wo_hbm, *refs
):
    out_ref, cos_ref, sin_ref, mask_ref, wa_ref, wo_ref, sem = refs
    rows, lanes = cos_ref.shape
    width = normed_ref.shape[1]
    blocks = width // lanes
    copies = []
    for n in range(blocks):
        here = slice(n * lanes, (n + 1) * lanes)
        for p in range(3):
            cols = slice(p * width + n * lanes, p * width + (n + 1) * lanes)
            copies.append(
                pltpu.make_async_copy(wa_hbm.at[:, cols], wa_ref.at[n, p], sem.at[4 * n + p])
            )
        copies.append(
            pltpu.make_async_copy(wo_hbm.at[here, :], wo_ref.at[here, :], sem.at[4 * n + 3])
        )
    for copy in copies:
        copy.start()

    def tables():
        ends = [info[ENDS + s : ENDS + s + 1, :] for s in range(SEQ_DEV)]
        place = lax.broadcasted_iota(jnp.int32, (rows, lanes), 0)
        index = slot_of(place, ends)
        start = jnp.zeros(place.shape, jnp.int32)
        terminal = jnp.zeros(place.shape, jnp.int32)
        offset = jnp.zeros(place.shape, jnp.int32)
        for s in range(SEQ_DEV):
            here = index == s
            start = jnp.where(here, info[STARTS + s : STARTS + s + 1, :], start)
            terminal = jnp.where(here, info[TERMS + s : TERMS + s + 1, :], terminal)
            offset = jnp.where(here, info[OFFS + s : OFFS + s + 1, :], offset)
        local = place - start
        position = jnp.where(local <= terminal, offset + local, local - terminal - 1)
        angle = position.astype(F32) * freq_ref[...]
        parity = lax.broadcasted_iota(jnp.int32, (rows, lanes), 1) % 2
        sine = jnp.sin(angle)
        cos_ref[...] = jnp.cos(angle)
        sin_ref[...] = jnp.where(parity == 0, -sine, sine)
        key = lax.broadcasted_iota(jnp.int32, (rows, rows), 0)
        query = lax.broadcasted_iota(jnp.int32, (rows, rows), 1)
        allowed = (slot_of(key, ends) == slot_of(query, ends)) & (key <= query)
        mask_ref[...] = jnp.where(allowed, 0.0, NEGATIVE)

    tables()
    even = lax.broadcasted_iota(jnp.int32, (rows, lanes), 1) % 2 == 0

    def swap(v):
        return jnp.where(even, pltpu.roll(v, lanes - 1, 1), pltpu.roll(v, 1, 1))

    def turn(v):
        return v * cos_ref[...] + swap(v) * sin_ref[...]

    def turn_back(v):
        return v * cos_ref[...] - swap(v) * sin_ref[...]

    scale = HEAD_DIM ** (-0.5)
    for n in range(blocks):
        for copy in copies[4 * n : 4 * n + 4]:
            copy.wait()
        here = slice(n * lanes, (n + 1) * lanes)
        attention_heads(
            normed_ref,
            bg_ref,
            wa_ref.at[n],
            wo_ref.at[here],
            mask_ref,
            [out_ref.at[m, :, here] for m in range(4)],
            turn,
            turn_back,
        )


def attention_heads(normed_ref, bg_ref, wa_ref, wo_ref, mask_ref, outs, turn, turn_back):
    rows, lanes = outs[0].shape
    scale = HEAD_DIM ** (-0.5)
    normed = normed_ref[...]
    queries = (turn(nn(normed, wa_ref[0])) * scale).astype(BF)
    keys = turn(nn(normed, wa_ref[1])).astype(BF)
    values = nn(normed, wa_ref[2]).astype(BF)
    grads = nt(bg_ref[...], wo_ref[...]).astype(BF)
    pair = 2 * HEAD_DIM
    lane = lax.broadcasted_iota(jnp.int32, (rows, pair), 1)
    masks = [lane < HEAD_DIM, lane >= HEAD_DIM]

    def one(v, h):
        return jnp.where(masks[h], v, jnp.zeros_like(v))

    queries_t = queries.T
    grads_t = grads.T
    keys_t = keys.T
    values_t = values.T
    attended_t, query_grad_t, key_grads, value_grads = [], [], [], []
    for p in range(lanes // pair):
        cols = slice(p * pair, (p + 1) * pair)
        q2, k2, v2, g2 = queries[:, cols], keys[:, cols], values[:, cols], grads[:, cols]
        scores2 = nn(jnp.concatenate([one(k2, 0), one(k2, 1)], axis=0), queries_t[cols, :])
        pg2 = nn(jnp.concatenate([one(v2, 0), one(v2, 1)], axis=0), grads_t[cols, :])
        key_grad = jnp.zeros((rows, pair), F32)
        value_grad = jnp.zeros((rows, pair), F32)
        for h in range(2):
            head = slice(p * pair + h * HEAD_DIM, p * pair + (h + 1) * HEAD_DIM)
            scores = scores2[h * rows : (h + 1) * rows] + mask_ref[...]
            exponent = jnp.exp(scores - jnp.max(scores, axis=0, keepdims=True))
            probs = exponent * (1.0 / jnp.sum(exponent, axis=0, keepdims=True))
            probs_low = probs.astype(BF)
            probs_grad = pg2[h * rows : (h + 1) * rows]
            row_dot = jnp.sum(probs * probs_grad, axis=0, keepdims=True)
            scores_grad = (probs * (probs_grad - row_dot)).astype(BF)
            attended_t.append(nn(values_t[head, :], probs_low))
            query_grad_t.append(nn(keys_t[head, :], scores_grad))
            key_grad = key_grad + nn(scores_grad, one(q2, h))
            value_grad = value_grad + nn(probs_low, one(g2, h))
        key_grads.append(key_grad)
        value_grads.append(value_grad)
    outs[0][...] = jnp.concatenate(attended_t, axis=0).T.astype(BF)
    outs[1][...] = turn_back(jnp.concatenate(query_grad_t, axis=0).T * scale).astype(BF)
    outs[2][...] = turn_back(jnp.concatenate(key_grads, axis=1)).astype(BF)
    outs[3][...] = jnp.concatenate(value_grads, axis=1).astype(BF)


def attention(info, normed, bg, attend_weight, output_weight, after=()):
    rows, width = normed.shape
    blocks = width // LANES
    pair = np.arange(LANES) % HEAD_DIM // 2
    freq = np.where(pair < ROT // 2, 10000.0 ** (-2.0 * pair / ROT), 0.0)[None].astype(np.float32)
    return call(
        attention_kernel,
        (info, normed, bg, jnp.asarray(freq), attend_weight, output_weight),
        struct((4, rows, width), BF),
        scratch=[
            pltpu.VMEM((rows, LANES), F32),
            pltpu.VMEM((rows, LANES), F32),
            pltpu.VMEM((rows, rows), F32),
            pltpu.VMEM((blocks, 3, width, LANES), BF),
            pltpu.VMEM((width, width), BF),
            pltpu.SemaphoreType.DMA((4 * blocks,)),
        ],
        specs={4: HBM, 5: HBM},
        vmem=52,
        after=after,
        tag="A",
    )


def attention_back_kernel(sides, wa_ref, wo_ref, grad_ref, out_ref):
    width = sides.shape[2]
    grad = nt(sides[1], wa_ref[:, :width])
    grad = grad + nt(sides[2], wa_ref[:, width : 2 * width])
    grad_ref[...] = grad + nt(sides[3], wa_ref[:, 2 * width :])
    out_ref[...] = nn(sides[0], wo_ref[...])


def attention_back(sides, attend_weight, output_weight, after=()):
    _, rows, width = sides.shape
    block = pl.BlockSpec((rows, LANES), lambda i: (0, i))
    specs = {
        0: pl.BlockSpec(sides.shape, lambda i: (0, 0, 0)),
        1: pl.BlockSpec((LANES, 3 * width), lambda i: (i, 0)),
        2: pl.BlockSpec((width, LANES), lambda i: (0, i)),
    }
    return call(
        attention_back_kernel,
        (sides, attend_weight, output_weight),
        (struct((rows, width), F32), struct((rows, width), F32)),
        specs=specs,
        out_specs=(block, block),
        grid=(width // LANES,),
        after=after,
        tag="B",
    )


def with_bit(n, bit):
    return [j for j in range(n) if j >> bit & 1]


def without_bit(n, bit):
    return [j for j in range(n) if not j >> bit & 1]


def attention_grads_kernel(
    chips, depth, n0, n1, g0, g1, s0, s1, ps, pk, qs, qk, ln, la, acc, sem
):
    rows, width = n0.shape
    chunk = width // chips
    half = chunk // 2
    cols = 4 * width // depth
    core, chip, zpos = places()
    for s, (tok, sb) in enumerate(((n0, s0), (n1, s1))):
        for k in range(chips):
            for ref, dst in ((tok, ln), (sb.at[0], la)):
                if half % 128 == 0:
                    start = pl.multiple_of(k * chunk + core * half, 128)
                    piece = ref[0:rows, pl.ds(start, half)]
                else:
                    both = ref[0:rows, k * chunk : (k + 1) * chunk].astype(F32)
                    piece = jnp.where(core == 0, both[:, :half], both[:, half:]).astype(BF)
                dst[k * half : (k + 1) * half, s * rows : (s + 1) * rows] = piece.T
    for a in range(depth):
        part, off = a * cols // width, a * cols % width
        span = slice(off, off + cols)
        if part < 3:
            left, right0, right1 = ln, s0[1 + part, :, span], s1[1 + part, :, span]
        else:
            left, right0, right1 = la, g0[:, span], g1[:, span]
        tile = (nn(left[:, :rows], right0) + nn(left[:, rows:], right1)).astype(BF)
        for k in range(chips):
            acc[chip ^ k, zpos ^ a] = tile[k * half : (k + 1) * half]
    mid = depth // 2
    copies = []
    top = chips.bit_length() - 2
    for js, dst, zs in (
        (with_bit(chips, 0), ps, slice(0, mid)),
        (without_bit(chips, 0), pk, slice(0, mid)),
        (with_bit(chips, top), qs, slice(mid, depth)),
        (without_bit(chips, top), qk, slice(mid, depth)),
    ):
        for i, j in enumerate(js):
            copies.append(pltpu.make_async_copy(acc.at[j, zs], dst.at[i], sem.at[len(copies)]))
    for copy in copies:
        copy.start()
    for copy in copies:
        copy.wait()


def attention_grads(chips, depth, own, core, s0, s1, after=()):
    rows, width = own[0].shape
    half = width // chips // 2
    cols = 4 * width // depth
    piece = struct((chips // 2, depth // 2, half, cols), BF)
    return call(
        partial(attention_grads_kernel, chips, depth),
        (own[0], core[0], own[1], core[1], s0, s1),
        (piece,) * 4,
        scratch=[
            pltpu.VMEM((chips * half, 2 * rows), BF),
            pltpu.VMEM((chips * half, 2 * rows), BF),
            pltpu.VMEM((chips, depth, half, cols), BF),
            pltpu.SemaphoreType.DMA((2 * chips,)),
        ],
        after=after,
        tag="A3",
    )


def load_weights(sources, we, ws, sem):
    hidden, width = ws.shape
    core, place, _ = places()
    if len(sources) == 2:
        half = pl.ds(pl.multiple_of(core * hidden, 128), hidden)
        return [
            pltpu.make_async_copy(sources[0].at[:, half], we, sem.at[0]),
            pltpu.make_async_copy(sources[1].at[half], ws, sem.at[1]),
        ]
    share, strip = hidden // len(sources), width // len(sources)
    copies = []
    for j, piece in enumerate(sources):
        chip = place ^ j
        copies.append(
            pltpu.make_async_copy(
                piece.at[pl.ds(0, strip), pl.ds(0, hidden)],
                we.at[pl.ds(pl.multiple_of(chip * strip, 16), strip)],
                sem.at[len(copies)],
            )
        )
        for b in range(width // hidden):
            copies.append(
                pltpu.make_async_copy(
                    piece.at[pl.ds(b * share, share), pl.ds(hidden, hidden)],
                    ws.at[
                        pl.ds(pl.multiple_of(chip * share, 16), share),
                        pl.ds(b * hidden, hidden),
                    ],
                    sem.at[len(copies)],
                )
            )
    return copies


def weight_scratch(chips, hidden, width):
    return [
        pltpu.VMEM((width, hidden), BF),
        pltpu.VMEM((hidden, width), BF),
        pltpu.SemaphoreType.DMA((chips * (1 + width // hidden),)),
    ]


def feed_kernel(chips, shards, pieces, *refs):
    toks, refs = refs[:8], refs[8:]
    sources = []
    for n in range(shards):
        size = chips if n else 2
        sources.append(refs[:size])
        refs = refs[size:]
    bias_ref, refs = refs[0], refs[1:]
    sums, keep, ps, pk, qs, qk = refs[:6]
    sends, refs = refs[6 : 6 + pieces], refs[6 + pieces :]
    x, bg, act_n, eg_n, act_t, eg_t, sem_in = refs[:7]
    refs = refs[7:]
    scratch = [refs[5 * n : 5 * n + 5] for n in range(shards)]
    rows, width = toks[0].shape
    hidden = act_t.shape[0] // shards
    loads = []
    for n, tok in enumerate(toks):
        dst = (x, bg)[n % 2].at[pl.ds(n // 2 * rows, rows)]
        loads.append(pltpu.make_async_copy(tok, dst, sem_in.at[n]))
    weights = []
    for n, (we, ws, sem, bias_rows, sem_b) in enumerate(scratch):
        copies = load_weights(sources[n], we, ws, sem)
        if n:
            strip = width // chips
            copies.append(
                pltpu.make_async_copy(sources[n][0].at[pl.ds(strip, BIAS_ROWS)], bias_rows, sem_b)
            )
        weights.append(copies)
    for copy in loads + [c for copies in weights for c in copies]:
        copy.start()
    for copy in loads:
        copy.wait()
    step = min(256, hidden)
    for n, (we, ws, _, bias_rows, _) in enumerate(scratch):
        for copy in weights[n]:
            copy.wait()
        if n:
            bias = jnp.sum(bias_rows[:, :hidden].astype(F32), axis=0, keepdims=True)
        else:
            bias = bias_ref[:, pl.ds(pl.multiple_of(places()[0] * hidden, 128), hidden)]
        for h in range(0, hidden, step):
            block = slice(h, h + step)
            there = slice(n * hidden + h, n * hidden + h + step)
            v = nn(x[...], we[:, block]) + bias[:, block]
            square = v * v
            t = jnp.tanh(0.7978845608 * v * (1.0 + 0.044715 * square))
            low = 0.5 * (1.0 + t)
            slope = low + 0.5 * v * (1.0 - t * t) * (0.7978845608 * (1.0 + 0.134145 * square))
            act = (v * low).astype(BF)
            eg = (nt(bg[...], ws[block, :]) * slope).astype(BF)
            act_n[:, there] = act
            eg_n[:, there] = eg
            act_t[there, :] = act.T
            eg_t[there, :] = eg.T
            sums[n : n + 1, block] = jnp.sum(eg.astype(F32), axis=0, keepdims=True)
    step = min(256, width)
    for c in range(0, width, step):
        block = slice(c, c + step)
        grad, out = 0.0, 0.0
        for n, (we, ws, _, _, _) in enumerate(scratch):
            part = slice(n * hidden, (n + 1) * hidden)
            grad = grad + nt(eg_n[:, part], we[block, :])
            out = out + nn(act_n[:, part], ws[:, block])
        for m, value in enumerate((grad, out)):
            for r in range(4):
                place, dst = (m, r // 2), keep
                if r % 2:
                    flat = 2 * m + r // 2
                    dst = sends[flat * pieces // 4]
                    place = {1: place, 2: place[1:], 4: ()}[pieces]
                dst[(*place, slice(None), block)] = value[r * rows : (r + 1) * rows].astype(BF)
    chunk = width // chips
    half = chunk // 2
    core, chip, _ = places()
    top = chips.bit_length() - 2

    def store(dst, i, tile, turned):
        for n in range(shards):
            for a in range(2):
                part = tile[n * hidden : (n + 1) * hidden, a * half : (a + 1) * half]
                dst[i, n, core ^ a] = part.T if turned else part

    for left, right, bit, go, stay in ((eg_t, x, 0, ps, pk), (act_t, bg, top, qs, qk)):
        for dst, js in ((go, with_bit(chips, bit)), (stay, without_bit(chips, bit))):
            for i, j in enumerate(js):
                if half % 128 == 0:
                    start = pl.multiple_of((chip ^ j) * chunk, 128)
                    store(dst, i, nn(left[...], right[:, pl.ds(start, chunk)]).astype(BF), False)
                    continue
                for k in range(chips):

                    @pl.when(chip ^ j == k)
                    def narrow():
                        span = slice(k * chunk, (k + 1) * chunk)
                        store(dst, i, nn(left[...], right[:, span]).astype(BF), True)


def feed(chips, toks, sources, bias, hidden, after=()):
    rows, width = toks[0].shape
    shards = len(sources)
    half = width // chips // 2
    edge = (hidden, half) if half % 128 == 0 else (half, hidden)
    piece = struct((chips // 2, shards, 2, *edge), BF)
    scratch = [pltpu.VMEM((4 * rows, width), BF)] * 2
    scratch += [pltpu.VMEM((4 * rows, shards * hidden), BF)] * 2
    scratch += [pltpu.VMEM((shards * hidden, 4 * rows), BF)] * 2
    scratch += [pltpu.SemaphoreType.DMA((8,))]
    for _ in range(shards):
        scratch += weight_scratch(chips, hidden, width)
        scratch += [pltpu.VMEM((BIAS_ROWS, 2 * hidden), BF), pltpu.SemaphoreType.DMA(())]
    args = (*toks, *[a for source in sources for a in source])
    specs = {n: ANY for n in range(len(args))}
    result = struct((2, 2, rows, width), BF)
    return call(
        partial(feed_kernel, chips, shards, CFG["send"]),
        (*args, bias),
        (struct((shards, hidden), F32), result)
        + (piece,) * 4
        + (struct({1: (2, 2, rows, width), 2: (2, rows, width), 4: (rows, width)}[CFG["send"]], BF),)
        * CFG["send"],
        scratch=scratch,
        specs=specs,
        vmem=36,
        tag="M",
        after=after,
    )


def norm_back_kernel(spot, info, x_ref, u_ref, gain_ref, g0, g1, g2, g3, sum_ref, biases, out_ref, small_ref):
    rows, width = x_ref.shape
    step = 64
    count = info[COUNT : COUNT + 1, 0:1].astype(F32)
    gain_sum = jnp.zeros((1, width), F32)
    shift_sum = jnp.zeros((1, width), F32)
    for r in range(0, rows, step):
        here = slice(r, r + step)
        xhat, inverse = normalize(x_ref[here, :].astype(F32))
        grad = g0[here, :] + g1[0, 0, here, :].astype(F32) + g2[(*spot, here)].astype(F32)
        grad = grad + g3[0, here, :].astype(F32)
        gain_sum = gain_sum + jnp.sum(grad * xhat, axis=0, keepdims=True)
        shift_sum = shift_sum + jnp.sum(grad, axis=0, keepdims=True)
        scaled = grad * gain_ref[...]
        mean = jnp.mean(scaled, axis=-1, keepdims=True)
        dot = jnp.mean(scaled * xhat, axis=-1, keepdims=True)
        out_ref[here, :] = u_ref[here, :].astype(F32) * count + inverse * (
            scaled - mean - xhat * dot
        )
    small_ref[...] = jnp.zeros(small_ref.shape, F32)
    small_ref[0:1, :] = gain_sum
    small_ref[1:2, :] = shift_sum
    small_ref[2:3, :] = sum_ref[...]
    small_ref[3:4, :] = jnp.zeros((1, width), F32) + count
    shards, hidden = biases.shape
    half = pl.ds(pl.multiple_of(places()[0] * hidden, 128), hidden)
    small_ref[SUMS : SUMS + shards, half] = biases[...]


def norm_back(info, x, u, gain, g0, g1, g2, g3, sums, biases, after=()):
    small = (SUMS + biases.shape[0], x.shape[1])
    return call(
        partial(norm_back_kernel, g2[1]),
        (info, x, u, gain, g0, g1, g2[0], g3, sums, biases),
        (struct(x.shape, F32), struct(small, F32)),
        after=after,
        tag="nb",
    )


def small_kernel(axis, bit, mine, other, out):
    if axis == "dp":
        out[...] = mine[...] + other[...]
        return
    out[:SUMS, :] = mine[:SUMS, :] + other[:SUMS, :]
    step = (1 << bit) // 2
    for k in range(mine.shape[0] - SUMS):
        row = slice(SUMS + k, SUMS + k + 1)
        if step and not k & step:
            twin = SUMS + (k | step)
            out[row, :] = mine[row, :] + other[twin : twin + 1, :]
        else:
            out[row, :] = mine[row, :]


def small_sum(small, axis, bit):
    other = exchange(small, axis, 1 << bit)
    return call(partial(small_kernel, axis, bit), (small, other), struct(small.shape, F32), tag="sm")


def row_out_kernel(spot, info, x_ref, sum_ref, g1, g2, g3, bias_ref, out_ref):
    rows, width = x_ref.shape
    step = 64
    for r in range(0, rows, step):
        here = slice(r, r + step)
        branch = sum_ref[here, :] + g1[1, 0, here, :].astype(F32) + g2[(*spot, here)].astype(F32)
        branch = branch + g3[g3.shape[0] - 1, here, :].astype(F32) + bias_ref[...]
        where = lax.broadcasted_iota(jnp.int32, (step, width), 0) + r
        branch = jnp.where(where < info[LIVE : LIVE + 1, 0:1], branch, 0.0)
        out_ref[here, :] = (x_ref[here, :].astype(F32) + branch).astype(BF)


def row_out(info, x, attention_out, g1, g2, g3, bias, after=()):
    return call(
        partial(row_out_kernel, g2[1]),
        (info, x, attention_out, g1, g2[0], g3, bias),
        struct(x.shape, BF),
        after=after,
        tag="ro",
    )


def attend_final_kernel(scale, picks, small_ref, *refs):
    parts, (attend, output) = refs[:-2], refs[-2:]
    depth = len(picks)
    cols = parts[0].shape[2]
    edge = 3 * depth // 4
    factor = scale / small_ref[3:4, 0:1]
    for j, (n, index) in picks.items():
        place = places()[2] ^ j
        value = parts[n][index].astype(F32) * factor

        @pl.when(place < edge)
        def inner():
            attend[:, pl.ds(pl.multiple_of(place * cols, 128), cols)] = value

        @pl.when(place >= edge)
        def outer():
            output[:, pl.ds(pl.multiple_of((place - edge) * cols, 128), cols)] = value


def attend_final(scale, small, have):
    arrays, picks = [], {}
    for j, (array, index) in have.items():
        n = next((n for n, a in enumerate(arrays) if a is array), len(arrays))
        if n == len(arrays):
            arrays.append(array)
        picks[j] = (n, index)
    _, half, cols = arrays[0].shape
    depth = len(picks)
    attend, output = (half, 3 * depth // 4 * cols), (half, depth // 4 * cols)
    return call(
        partial(attend_final_kernel, scale, picks),
        (small, *arrays),
        (struct(attend, F32), struct(output, F32)),
        tag="af",
    )


def row_final_kernel(scale, small_ref, grad_ref, out_ref, gain, shift, bias, expand):
    factor = scale / small_ref[3:4, 0:1]
    out_ref[...] = grad_ref[...] * factor
    gain[...] = small_ref[0:1, :] * factor
    shift[...] = small_ref[1:2, :] * factor
    bias[...] = small_ref[2:3, :] * factor
    expand[...] = small_ref[SUMS : SUMS + 1, : expand.shape[1]] * factor


def row_final(scale, small, grad, shard):
    row = struct((1, grad.shape[1]), F32)
    return call(
        partial(row_final_kernel, scale),
        (small, grad),
        (struct(grad.shape, F32), row, row, row, struct((1, shard), F32)),
        tag="rf",
    )


def feed_final_kernel(scale, narrow, small_ref, mine, sibling, expand, shrink):
    hidden = mine.shape[2 if narrow else 1]
    factor = scale / small_ref[3:4, 0:1]
    for n, part in enumerate((mine, sibling)):
        start = pl.multiple_of((places()[0] ^ n) * hidden, 128)
        first, second = part[0].astype(F32), part[1].astype(F32)
        expand[:, pl.ds(start, hidden)] = (first if narrow else first.T) * factor
        shrink[pl.ds(start, hidden), :] = (second.T if narrow else second) * factor


def feed_final(scale, small, mine, sibling, half):
    narrow = half % 128 != 0
    hidden = mine.shape[2 if narrow else 1]
    return call(
        partial(feed_final_kernel, scale, narrow),
        (small, mine, sibling),
        (struct((half, 2 * hidden), F32), struct((2 * hidden, half), F32)),
        tag="ff",
    )


def add_kernel(plan, *refs):
    ins = refs[: len(refs) - len(plan)]
    for out, (_, parts) in zip(refs[len(ins) :], plan):
        for p, part in enumerate(parts):
            out[p] = sum(ins[n][index].astype(F32) for n, index in part).astype(out.dtype)


def add(plan, tag, after=()):
    arrays, outs, inner = [], [], []
    for dtype, parts in plan:
        entries = []
        for part in parts:
            entry = []
            for array, index in part:
                n = next((n for n, a in enumerate(arrays) if a is array), len(arrays))
                if n == len(arrays):
                    arrays.append(array)
                entry.append((n, index))
            entries.append(entry)
        inner.append((dtype, entries))
        array, index = parts[0][0]
        outs.append(struct((len(parts), *array.shape[len(index) :]), dtype))
    return call(partial(add_kernel, inner), tuple(arrays), tuple(outs), tag=tag, after=after)


def exchange(x, axis, flip):
    n = lax.axis_size(axis)
    return lax.ppermute(x, axis, [(i, i ^ flip) for i in range(n)])


def reduce_chips(chips, low, high, tag, afters=()):
    bits = list(range(chips.bit_length() - 1))
    orders = (bits, bits[::-1])
    left = []
    for (send, keep), order in zip((low, high), orders):
        got = exchange(send, "dp", 2 << order[0])
        left.append([[(keep, (i,)), (got, (i,))] for i in range(chips // 2)])
    sends = ()
    for n in range(1, len(bits)):
        stay, go = [], []
        for entries, order in zip(left, orders):
            if order[0] == 0:
                stay.append(entries[0::2])
                go.append(entries[1::2])
            else:
                stay.append(entries[: len(entries) // 2])
                go.append(entries[len(entries) // 2 :])
        sends = add([(BF, g) for g in go], tag, after=afters)
        left = []
        for entries, send, order in zip(stay, sends, orders):
            got = exchange(send, "dp", 2 << order[n])
            left.append([e + [(got, (i,))] for i, e in enumerate(entries)])
    return (left[0][0], left[1][0]), sends


def behind(x, *others):
    return lax.optimization_barrier((x, *others))[0]


def reduce_depth(parts, entries, depth):
    left = {j: e for j, e in enumerate(entries)}
    for bit in range(depth.bit_length() - 1):
        go = [j for j in left if j >> bit & 1]
        if bit:
            parts = add([(BF, [left[j] for j in go])], "zadd")[0]
        got = exchange(parts, "mp", 1 << bit)
        for n, j in enumerate(go):
            left[j ^ (1 << bit)] = left[j ^ (1 << bit)] + [(got, (n,))]
            del left[j]
    return left[0]


def gather_depth(own, depth):
    have = {0: (own, (0,))}
    packed = own
    for bit in reversed(range(depth.bit_length() - 1)):
        order = list(have)
        if len(order) > 1:
            packed = add([(BF, [[have[j]] for j in order])], "zjoin")[0]
        got = exchange(packed, "mp", 1 << bit)
        for n, j in enumerate(order):
            have[j ^ (1 << bit)] = (got, (n,))
    return have


def at(entry, *index):
    return [(array, first + index) for array, first in entry]


def local(
    residual_in,
    upstream,
    layer_norm_gain,
    layer_norm_bias,
    attend_weight,
    output_weight,
    expand_weight,
    expand_bias,
    shrink_weight,
    shrink_bias,
    seq_lengths,
    terminal_pos,
    window_offset,
):
    rows, width = residual_in.shape
    data_ways, depth = lax.axis_size("dp"), lax.axis_size("mp")
    chips = data_ways // 2
    shards = depth // 2
    shard = expand_weight.shape[1]
    hidden = shard // 2
    gain = layer_norm_gain[None, :]
    packed = pack(chips, expand_bias[None, :], expand_weight, shrink_weight)
    shares = [exchange(packed, "mp", 2 * k) for k in range(1, shards)]
    info, normed, bg, shrink_bias_grad = prepare(
        seq_lengths,
        terminal_pos,
        window_offset,
        residual_in,
        upstream,
        gain,
        layer_norm_bias[None, :],
        after=(packed,),
    )
    tok = (normed, bg)
    tok_core = [exchange(t, "dp", 1) for t in tok]

    sides = attention(info, normed, bg, attend_weight, output_weight)
    grad_attention, attention_out = attention_back(sides, attend_weight, output_weight)
    deep_normed = exchange(behind(normed, sides) if CFG["deep0"] else normed, "mp", 1)
    wait = []
    if CFG["sidesB"]:
        wait.append(grad_attention)
    if CFG["sidesS"]:
        wait += shares
    if CFG["sidesC"]:
        wait += tok_core
    if CFG["sidesD"]:
        wait.append(deep_normed)
    sides_core = exchange(behind(sides, *wait) if wait else sides, "dp", 1)
    hold = {0: (), 1: (sides,), 2: (deep_normed,), 3: (grad_attention,), 4: tuple(shares)}[CFG["deep1"]]
    tok_deep = [deep_normed, exchange(behind(bg, *hold) if hold else bg, "mp", 1)]
    hold = {0: (), 1: (sides,), 2: (grad_attention,), 3: (sides_core,)}[CFG["W2"]]
    held = [behind(s, *hold) if hold else s for s in shares]
    foreign = [[s] + [exchange(s, "dp", 2 * j) for j in range(1, chips)] for s in held]
    attn = attention_grads(
        chips, depth, tok, tok_core, sides, sides_core, after={0: (), 1: shares, 2: (*shares, grad_attention)}[CFG["A3S"]]
    )
    hold = {0: (), 1: (attn[0],), 2: (sides,), 3: (sides_core,)}[CFG["bothA3"]]
    tok_both = [exchange(behind(t, *hold) if hold else t, "dp", 1) for t in tok_deep]
    if CFG["attnBoth"]:
        attn = [behind(a, *tok_both) for a in attn]
    toks = (*tok, *tok_core, *tok_deep, *tok_both)

    fed = feed(
        chips,
        toks,
        [(expand_weight, shrink_weight), *foreign],
        expand_bias[None, :],
        hidden,
        after=attn[:1] if CFG["MA3"] else (),
    )
    sums, keep = fed[:2]
    got = [exchange(f, "dp", 1) for f in fed[6:]]

    def passed(m, r):
        return {1: (got[0], (m, r)), 2: (got[m % len(got)], (r,)), 4: (got[-1 if len(got) < 4 else 2 * m + r], ())}[len(got)]

    entries = [[(keep, (m, 1)), passed(m, 1)] for m in range(2)]
    if CFG["cross2"]:
        crossing = add([(BF, [e]) for e in entries], "cross")
        crossed = [exchange(c, "mp", 1) for c in crossing]
    else:
        crossing = add([(BF, entries)], "cross")
        crossed = [exchange(crossing[0], "mp", 1)]

    hold = {0: (), 1: (keep,), 2: (crossing[0],)}[CFG["at1"]]
    tracks, attn_sent = reduce_chips(chips, attn[:2], attn[2:], "at1", hold)
    middle = depth // 2
    entries = [at(tracks[z // middle], z % middle) for z in range(depth)]

    def feed_sums():
        hold = {0: (), 1: (attn_sent[0],), 2: (crossing[0],), 3: (attn_sent[0], crossing[0])}[CFG["fo1"]]
        return reduce_chips(chips, fed[2:4], fed[4:6], "fo1", hold)

    def rows_back(after):
        return norm_back(
            info,
            residual_in,
            upstream,
            gain,
            grad_attention,
            keep,
            passed(0, 0),
            crossed[0],
            shrink_bias_grad,
            sums,
            after=after,
        )

    def attention_parts(after):
        return add([(BF, [e for j, e in enumerate(entries) if j & 1])], "parts", after=after)

    mine, away = [[], []], [[], []]
    if CFG["nb"] == 1:
        grad_rows, small = rows_back(())
    if CFG["first"]:
        parts = attention_parts((small,) if CFG["nb"] == 1 and CFG["parts"] else ())
        pair, sent = feed_sums()
    else:
        pair, sent = feed_sums()
        parts = attention_parts({0: (), 1: (sent[0],), 2: (small,) if CFG["nb"] == 1 else ()}[CFG["parts"]])
    if CFG["nb"] != 1:
        grad_rows, small = rows_back((parts[0],) if CFG["nb"] else ())
    hold = {0: (), 1: (parts[0],), 2: (small,)}[CFG["both"]]
    for k in range(1, shards):
        both = add([(BF, [at(p, k, a) for p in pair for a in range(2)])], "both", after=hold)[0]
        both = exchange(both, "mp", 2 * k)
        for n in range(2):
            mine[n].append((both, (2 * n,)))
            away[n].append((both, (2 * n + 1,)))
    if CFG["nb"] == 3:
        pass
    attn_own = add([(BF, [reduce_depth(parts[0], entries, depth)])], "aown")[0]
    attn_all = gather_depth(attn_own, depth)
    for n in range(2):
        mine[n] += at(pair[n], 0, 0)
        away[n] += at(pair[n], 0, 1)
    mine, away = add([(F32, mine), (BF, away)], "mine")
    sibling = exchange(away, "dp", 1)

    residual_out = row_out(
        info, residual_in, attention_out, keep, passed(1, 0), crossed[-1], shrink_bias[None, :]
    )
    for bit in range(depth.bit_length() - 1):
        small = small_sum(small, "mp", bit)
    for bit in range(data_ways.bit_length() - 1):
        small = small_sum(small, "dp", bit)

    factor = float(data_ways * depth)
    attend_sum, output_sum = attend_final(factor, small, attn_all)
    expand_sum, shrink_sum = feed_final(factor, small, mine, sibling, width // data_ways)
    grad_rows, gain_sum, shift_sum, bias_sum, expand_bias_sum = row_final(
        factor, small, grad_rows, shard
    )
    return (
        residual_out,
        grad_rows,
        gain_sum[0],
        shift_sum[0],
        attend_sum,
        output_sum,
        expand_sum,
        expand_bias_sum[0],
        shrink_sum,
        bias_sum[0],
    )


def solution(mesh):
    in_specs = (
        P(("dp", "mp"), None),
        P(("dp", "mp"), None),
        P(),
        P(),
        P(),
        P(),
        P(None, "mp"),
        P("mp"),
        P("mp", None),
        P(),
        P("dp", None),
        P("dp", "mp"),
        P("dp", "mp"),
    )
    out_specs = (
        P(("dp", "mp"), None),
        P(("dp", "mp"), None),
        P(),
        P(),
        P("dp", None),
        P("dp", None),
        P("dp", "mp"),
        P("mp"),
        P("mp", "dp"),
        P(),
    )
    return jax.shard_map(local, mesh=mesh, in_specs=in_specs, out_specs=out_specs, check_vma=False)
```

```python
from functools import partial

import numpy as np

import jax
import jax.numpy as jnp
from jax import lax
from jax.experimental import pallas as pl
from jax.experimental.pallas import tpu as pltpu
from jax.sharding import PartitionSpec as P

HEADS = 16
HEAD_DIM = 64
ROT = 32
SEQ_DEV = 4
EPSILON = 1e-05
NEGATIVE = -1e30
LANES = 256
BF = jnp.bfloat16
F32 = jnp.float32
MIB = 1 << 20
BIAS_ROWS = 16
COST = {'pack': 3, 'prep': 1, 'A': 0.05, 'B': 1, 'A3': 25, 'M': 50, 'cross': 0.3, 'at1': 12, 'fo1': 0.05, 'both': 6, 'parts': 0.05, 'aown': 0.05, 'mine': 3, 'nb': 1, 'ro': 12, 'sm': 6, 'af': 50, 'rf': 25, 'ff': 1, 'zadd': 6, 'zjoin': 1}
CFG = {'deep0': 1, 'deep1': 4, 'sidesB': 1, 'sidesS': 1, 'sidesC': 1, 'sidesD': 0, 'W2': 1, 'A3S': 2, 'bothA3': 1, 'attnBoth': 1, 'MA3': 1, 'cross2': 1, 'at1': 1, 'fo1': 3, 'first': 0, 'nb': 1, 'parts': 0, 'both': 1, 'send': 1}
SUMS = 4

COUNT, LIVE, ENDS, STARTS, TERMS, OFFS, TABLE = 0, 1, 2, 6, 10, 14, 24


def nn(a, b):
    return lax.dot_general(a, b, (((1,), (0,)), ((), ())), preferred_element_type=F32)


def nt(a, b):
    return lax.dot_general(a, b, (((1,), (1,)), ((), ())), preferred_element_type=F32)


def call(kernel, args, outs, scratch=(), specs=None, out_specs=None, grid=None, vmem=24, tag="", after=()):
    count = len(args)
    specs = specs or {}

    def body(*refs):
        kernel(*refs[:count], *refs[count + len(after) :])

    single = not isinstance(outs, tuple)
    options = {} if grid is None else {"grid": grid}
    return pl.pallas_call(
        body,
        in_specs=[specs.get(n, VMEM) for n in range(count)] + [ANY] * len(after),
        out_specs=out_specs or (VMEM if single else (VMEM,) * len(outs)),
        out_shape=outs,
        scratch_shapes=list(scratch),
        compiler_params=pltpu.CompilerParams(vmem_limit_bytes=vmem * MIB),
        cost_estimate=pl.CostEstimate(
            flops=int(COST[tag] * 1e9), bytes_accessed=1024, transcendentals=0
        ),
        **options,
    )(*args, *after)


def places():
    place = lax.axis_index("dp")
    return lax.bitwise_and(place, 1), lax.shift_right_logical(place, 1), lax.axis_index("mp")


VMEM = pl.BlockSpec(memory_space=pltpu.VMEM)
SMEM = pl.BlockSpec(memory_space=pltpu.SMEM)
HBM = pl.BlockSpec(memory_space=pltpu.HBM)
ANY = pl.BlockSpec(memory_space=pl.ANY)


def struct(shape, dtype):
    return jax.ShapeDtypeStruct(shape, dtype)


def normalize(hidden):
    mean = jnp.mean(hidden, axis=-1, keepdims=True)
    removed = hidden - mean
    variance = jnp.mean(removed * removed, axis=-1, keepdims=True)
    inverse = lax.rsqrt(variance + EPSILON)
    return removed * inverse, inverse


def pack_kernel(chips, eb_ref, we_ref, ws_ref, pack_ref, row_ref, sem):
    width = we_ref.shape[0]
    hidden = ws_ref.shape[0] // 2
    share, strip = hidden // chips, width // chips
    core, chip, _ = places()
    half = pl.ds(pl.multiple_of(core * hidden, 128), hidden)
    start = pl.multiple_of(core * hidden + chip * share, 16)
    copies = [
        pltpu.make_async_copy(eb_ref.at[:, half], row_ref, sem.at[0]),
        pltpu.make_async_copy(
            we_ref.at[pl.ds(pl.multiple_of(chip * strip, 16), strip), half],
            pack_ref.at[pl.ds(0, strip), pl.ds(0, hidden)],
            sem.at[1],
        ),
    ]
    for b in range(width // hidden):
        copies.append(
            pltpu.make_async_copy(
                ws_ref.at[pl.ds(start, share), pl.ds(b * hidden, hidden)],
                pack_ref.at[pl.ds(b * share, share), pl.ds(hidden, hidden)],
                sem.at[2 + b],
            )
        )
    for copy in copies:
        copy.start()
    copies[0].wait()
    bias = row_ref[...]
    high = bias.astype(BF)
    middle = (bias - high.astype(F32)).astype(BF)
    lowest = (bias - high.astype(F32) - middle.astype(F32)).astype(BF)
    line = lax.broadcasted_iota(jnp.int32, (BIAS_ROWS, hidden), 0)
    table = jnp.where(line == 0, high.astype(F32), 0.0)
    table = jnp.where(line == 1, middle.astype(F32), table)
    table = jnp.where(line == 2, lowest.astype(F32), table)
    pack_ref[strip:, :hidden] = table.astype(BF)
    pack_ref[strip:, hidden:] = jnp.zeros((BIAS_ROWS, hidden), BF)
    for copy in copies[1:]:
        copy.wait()


def pack(chips, eb, we, ws):
    width, hidden = we.shape[0], ws.shape[0] // 2
    return call(
        partial(pack_kernel, chips),
        (eb, we, ws),
        struct((width // chips + BIAS_ROWS, 2 * hidden), BF),
        scratch=[
            pltpu.VMEM((1, hidden), F32),
            pltpu.SemaphoreType.DMA((2 + width // hidden,)),
        ],
        specs={0: HBM, 1: HBM, 2: HBM},
        vmem=59,
        tag="pack",
    )


def prepare_kernel(
    lens_ref,
    terms_ref,
    offs_ref,
    x_hbm,
    u_hbm,
    gain_hbm,
    bias_hbm,
    info,
    normed_ref,
    grad_ref,
    sum_ref,
    x_ref,
    u_ref,
    gain_ref,
    bias_ref,
    sem,
):
    rows, width = x_ref.shape
    zpos = places()[2]
    copies = [
        pltpu.make_async_copy(src, dst, sem.at[n])
        for n, (src, dst) in enumerate(
            ((x_hbm, x_ref), (gain_hbm, gain_ref), (bias_hbm, bias_ref), (u_hbm, u_ref))
        )
    ]
    for copy in copies:
        copy.start()

    def note(row, number):
        info[row : row + 1, :] = jnp.zeros((1, info.shape[1]), jnp.int32) + number

    live = 0
    for s in range(SEQ_DEV):
        note(STARTS + s, live)
        live = live + lens_ref[0, zpos * SEQ_DEV + s]
        note(ENDS + s, live)
        note(TERMS + s, terms_ref[0, s])
        note(OFFS + s, offs_ref[0, s])
    total = 0
    for s in range(lens_ref.shape[1]):
        total = total + lens_ref[0, s]
    note(LIVE, live)
    note(COUNT, total)
    step = 64
    count = total.astype(F32)
    sums = jnp.zeros((1, width), F32)
    for copy in copies:
        copy.wait()
    for r in range(0, rows, step):
        xhat, _ = normalize(x_ref[r : r + step, :].astype(F32))
        normed_ref[r : r + step, :] = (xhat * gain_ref[...] + bias_ref[...]).astype(BF)
        where = lax.broadcasted_iota(jnp.int32, (step, width), 0) + r
        grad = jnp.where(where < live, u_ref[r : r + step, :].astype(F32) * count, 0.0).astype(BF)
        grad_ref[r : r + step, :] = grad
        sums = sums + jnp.sum(grad.astype(F32), axis=0, keepdims=True)
    sum_ref[...] = sums


def prepare(lens, terms, offs, x, u, gain, bias, after=()):
    rows, width = x.shape
    return call(
        prepare_kernel,
        (lens, terms, offs, x, u, gain, bias),
        (
            struct((TABLE, LANES), jnp.int32),
            struct((rows, width), BF),
            struct((rows, width), BF),
            struct((1, width), F32),
        ),
        scratch=[
            pltpu.VMEM((rows, width), BF),
            pltpu.VMEM((rows, width), BF),
            pltpu.VMEM((1, width), F32),
            pltpu.VMEM((1, width), F32),
            pltpu.SemaphoreType.DMA((4,)),
        ],
        specs={0: SMEM, 1: SMEM, 2: SMEM, 3: HBM, 4: HBM, 5: HBM, 6: HBM},
        vmem=57,
        after=after,
        tag="prep",
    )


def slot_of(place, ends):
    index = jnp.zeros(place.shape, jnp.int32)
    for end in ends:
        index = index + (place >= end).astype(jnp.int32)
    return index


def attention_kernel(
    info, normed_ref, bg_ref, freq_ref, wa_hbm, wo_hbm, *refs
):
    out_ref, cos_ref, sin_ref, mask_ref, wa_ref, wo_ref, sem = refs
    rows, lanes = cos_ref.shape
    width = normed_ref.shape[1]
    blocks = width // lanes
    copies = []
    for n in range(blocks):
        here = slice(n * lanes, (n + 1) * lanes)
        for p in range(3):
            cols = slice(p * width + n * lanes, p * width + (n + 1) * lanes)
            copies.append(
                pltpu.make_async_copy(wa_hbm.at[:, cols], wa_ref.at[n, p], sem.at[4 * n + p])
            )
        copies.append(
            pltpu.make_async_copy(wo_hbm.at[here, :], wo_ref.at[here, :], sem.at[4 * n + 3])
        )
    for copy in copies:
        copy.start()

    def tables():
        ends = [info[ENDS + s : ENDS + s + 1, :] for s in range(SEQ_DEV)]
        place = lax.broadcasted_iota(jnp.int32, (rows, lanes), 0)
        index = slot_of(place, ends)
        start = jnp.zeros(place.shape, jnp.int32)
        terminal = jnp.zeros(place.shape, jnp.int32)
        offset = jnp.zeros(place.shape, jnp.int32)
        for s in range(SEQ_DEV):
            here = index == s
            start = jnp.where(here, info[STARTS + s : STARTS + s + 1, :], start)
            terminal = jnp.where(here, info[TERMS + s : TERMS + s + 1, :], terminal)
            offset = jnp.where(here, info[OFFS + s : OFFS + s + 1, :], offset)
        local = place - start
        position = jnp.where(local <= terminal, offset + local, local - terminal - 1)
        angle = position.astype(F32) * freq_ref[...]
        parity = lax.broadcasted_iota(jnp.int32, (rows, lanes), 1) % 2
        sine = jnp.sin(angle)
        cos_ref[...] = jnp.cos(angle)
        sin_ref[...] = jnp.where(parity == 0, -sine, sine)
        key = lax.broadcasted_iota(jnp.int32, (rows, rows), 0)
        query = lax.broadcasted_iota(jnp.int32, (rows, rows), 1)
        allowed = (slot_of(key, ends) == slot_of(query, ends)) & (key <= query)
        mask_ref[...] = jnp.where(allowed, 0.0, NEGATIVE)

    tables()
    even = lax.broadcasted_iota(jnp.int32, (rows, lanes), 1) % 2 == 0

    def swap(v):
        return jnp.where(even, pltpu.roll(v, lanes - 1, 1), pltpu.roll(v, 1, 1))

    def turn(v):
        return v * cos_ref[...] + swap(v) * sin_ref[...]

    def turn_back(v):
        return v * cos_ref[...] - swap(v) * sin_ref[...]

    scale = HEAD_DIM ** (-0.5)
    for n in range(blocks):
        for copy in copies[4 * n : 4 * n + 4]:
            copy.wait()
        here = slice(n * lanes, (n + 1) * lanes)
        attention_heads(
            normed_ref,
            bg_ref,
            wa_ref.at[n],
            wo_ref.at[here],
            mask_ref,
            [out_ref.at[m, :, here] for m in range(4)],
            turn,
            turn_back,
        )


def attention_heads(normed_ref, bg_ref, wa_ref, wo_ref, mask_ref, outs, turn, turn_back):
    rows, lanes = outs[0].shape
    scale = HEAD_DIM ** (-0.5)
    normed = normed_ref[...]
    queries = (turn(nn(normed, wa_ref[0])) * scale).astype(BF)
    keys = turn(nn(normed, wa_ref[1])).astype(BF)
    values = nn(normed, wa_ref[2]).astype(BF)
    grads = nt(bg_ref[...], wo_ref[...]).astype(BF)
    pair = 2 * HEAD_DIM
    lane = lax.broadcasted_iota(jnp.int32, (rows, pair), 1)
    masks = [lane < HEAD_DIM, lane >= HEAD_DIM]

    def one(v, h):
        return jnp.where(masks[h], v, jnp.zeros_like(v))

    queries_t = queries.T
    grads_t = grads.T
    keys_t = keys.T
    values_t = values.T
    attended_t, query_grad_t, key_grads, value_grads = [], [], [], []
    for p in range(lanes // pair):
        cols = slice(p * pair, (p + 1) * pair)
        q2, k2, v2, g2 = queries[:, cols], keys[:, cols], values[:, cols], grads[:, cols]
        scores2 = nn(jnp.concatenate([one(k2, 0), one(k2, 1)], axis=0), queries_t[cols, :])
        pg2 = nn(jnp.concatenate([one(v2, 0), one(v2, 1)], axis=0), grads_t[cols, :])
        key_grad = jnp.zeros((rows, pair), F32)
        value_grad = jnp.zeros((rows, pair), F32)
        for h in range(2):
            head = slice(p * pair + h * HEAD_DIM, p * pair + (h + 1) * HEAD_DIM)
            scores = scores2[h * rows : (h + 1) * rows] + mask_ref[...]
            exponent = jnp.exp(scores - jnp.max(scores, axis=0, keepdims=True))
            probs = exponent * (1.0 / jnp.sum(exponent, axis=0, keepdims=True))
            probs_low = probs.astype(BF)
            probs_grad = pg2[h * rows : (h + 1) * rows]
            row_dot = jnp.sum(probs * probs_grad, axis=0, keepdims=True)
            scores_grad = (probs * (probs_grad - row_dot)).astype(BF)
            attended_t.append(nn(values_t[head, :], probs_low))
            query_grad_t.append(nn(keys_t[head, :], scores_grad))
            key_grad = key_grad + nn(scores_grad, one(q2, h))
            value_grad = value_grad + nn(probs_low, one(g2, h))
        key_grads.append(key_grad)
        value_grads.append(value_grad)
    outs[0][...] = jnp.concatenate(attended_t, axis=0).T.astype(BF)
    outs[1][...] = turn_back(jnp.concatenate(query_grad_t, axis=0).T * scale).astype(BF)
    outs[2][...] = turn_back(jnp.concatenate(key_grads, axis=1)).astype(BF)
    outs[3][...] = jnp.concatenate(value_grads, axis=1).astype(BF)


def attention(info, normed, bg, attend_weight, output_weight, after=()):
    rows, width = normed.shape
    blocks = width // LANES
    pair = np.arange(LANES) % HEAD_DIM // 2
    freq = np.where(pair < ROT // 2, 10000.0 ** (-2.0 * pair / ROT), 0.0)[None].astype(np.float32)
    return call(
        attention_kernel,
        (info, normed, bg, jnp.asarray(freq), attend_weight, output_weight),
        struct((4, rows, width), BF),
        scratch=[
            pltpu.VMEM((rows, LANES), F32),
            pltpu.VMEM((rows, LANES), F32),
            pltpu.VMEM((rows, rows), F32),
            pltpu.VMEM((blocks, 3, width, LANES), BF),
            pltpu.VMEM((width, width), BF),
            pltpu.SemaphoreType.DMA((4 * blocks,)),
        ],
        specs={4: HBM, 5: HBM},
        vmem=56,
        after=after,
        tag="A",
    )


def attention_back_kernel(sides, wa_ref, wo_ref, grad_ref, out_ref):
    width = sides.shape[2]
    grad = nt(sides[1], wa_ref[:, :width])
    grad = grad + nt(sides[2], wa_ref[:, width : 2 * width])
    grad_ref[...] = grad + nt(sides[3], wa_ref[:, 2 * width :])
    out_ref[...] = nn(sides[0], wo_ref[...])


def attention_back(sides, attend_weight, output_weight, after=()):
    _, rows, width = sides.shape
    block = pl.BlockSpec((rows, LANES), lambda i: (0, i))
    specs = {
        0: pl.BlockSpec(sides.shape, lambda i: (0, 0, 0)),
        1: pl.BlockSpec((LANES, 3 * width), lambda i: (i, 0)),
        2: pl.BlockSpec((width, LANES), lambda i: (0, i)),
    }
    return call(
        attention_back_kernel,
        (sides, attend_weight, output_weight),
        (struct((rows, width), F32), struct((rows, width), F32)),
        specs=specs,
        out_specs=(block, block),
        grid=(width // LANES,),
        after=after,
        tag="B",
    )


def with_bit(n, bit):
    return [j for j in range(n) if j >> bit & 1]


def without_bit(n, bit):
    return [j for j in range(n) if not j >> bit & 1]


def attention_grads_kernel(
    chips, depth, n0, n1, g0, g1, s0, s1, ps, pk, qs, qk, ln, la, acc, sem
):
    rows, width = n0.shape
    chunk = width // chips
    half = chunk // 2
    cols = 4 * width // depth
    core, chip, zpos = places()
    for s, (tok, sb) in enumerate(((n0, s0), (n1, s1))):
        for k in range(chips):
            for ref, dst in ((tok, ln), (sb.at[0], la)):
                if half % 128 == 0:
                    start = pl.multiple_of(k * chunk + core * half, 128)
                    piece = ref[0:rows, pl.ds(start, half)]
                else:
                    both = ref[0:rows, k * chunk : (k + 1) * chunk].astype(F32)
                    piece = jnp.where(core == 0, both[:, :half], both[:, half:]).astype(BF)
                dst[k * half : (k + 1) * half, s * rows : (s + 1) * rows] = piece.T
    for a in range(depth):
        part, off = a * cols // width, a * cols % width
        span = slice(off, off + cols)
        if part < 3:
            left, right0, right1 = ln, s0[1 + part, :, span], s1[1 + part, :, span]
        else:
            left, right0, right1 = la, g0[:, span], g1[:, span]
        tile = (nn(left[:, :rows], right0) + nn(left[:, rows:], right1)).astype(BF)
        for k in range(chips):
            acc[chip ^ k, zpos ^ a] = tile[k * half : (k + 1) * half]
    mid = depth // 2
    copies = []
    top = chips.bit_length() - 2
    for js, dst, zs in (
        (with_bit(chips, 0), ps, slice(0, mid)),
        (without_bit(chips, 0), pk, slice(0, mid)),
        (with_bit(chips, top), qs, slice(mid, depth)),
        (without_bit(chips, top), qk, slice(mid, depth)),
    ):
        for i, j in enumerate(js):
            copies.append(pltpu.make_async_copy(acc.at[j, zs], dst.at[i], sem.at[len(copies)]))
    for copy in copies:
        copy.start()
    for copy in copies:
        copy.wait()


def attention_grads(chips, depth, own, core, s0, s1, after=()):
    rows, width = own[0].shape
    half = width // chips // 2
    cols = 4 * width // depth
    piece = struct((chips // 2, depth // 2, half, cols), BF)
    return call(
        partial(attention_grads_kernel, chips, depth),
        (own[0], core[0], own[1], core[1], s0, s1),
        (piece,) * 4,
        scratch=[
            pltpu.VMEM((chips * half, 2 * rows), BF),
            pltpu.VMEM((chips * half, 2 * rows), BF),
            pltpu.VMEM((chips, depth, half, cols), BF),
            pltpu.SemaphoreType.DMA((2 * chips,)),
        ],
        after=after,
        tag="A3",
    )


def load_weights(sources, we, ws, sem):
    hidden, width = ws.shape
    core, place, _ = places()
    if len(sources) == 2:
        half = pl.ds(pl.multiple_of(core * hidden, 128), hidden)
        return [
            pltpu.make_async_copy(sources[0].at[:, half], we, sem.at[0]),
            pltpu.make_async_copy(sources[1].at[half], ws, sem.at[1]),
        ]
    share, strip = hidden // len(sources), width // len(sources)
    copies = []
    for j, piece in enumerate(sources):
        chip = place ^ j
        copies.append(
            pltpu.make_async_copy(
                piece.at[pl.ds(0, strip), pl.ds(0, hidden)],
                we.at[pl.ds(pl.multiple_of(chip * strip, 16), strip)],
                sem.at[len(copies)],
            )
        )
        for b in range(width // hidden):
            copies.append(
                pltpu.make_async_copy(
                    piece.at[pl.ds(b * share, share), pl.ds(hidden, hidden)],
                    ws.at[
                        pl.ds(pl.multiple_of(chip * share, 16), share),
                        pl.ds(b * hidden, hidden),
                    ],
                    sem.at[len(copies)],
                )
            )
    return copies


def weight_scratch(chips, hidden, width):
    return [
        pltpu.VMEM((width, hidden), BF),
        pltpu.VMEM((hidden, width), BF),
        pltpu.SemaphoreType.DMA((chips * (1 + width // hidden),)),
    ]


def feed_kernel(chips, shards, pieces, *refs):
    toks, refs = refs[:8], refs[8:]
    sources = []
    for n in range(shards):
        size = chips if n else 2
        sources.append(refs[:size])
        refs = refs[size:]
    bias_ref, refs = refs[0], refs[1:]
    sums, keep, ps, pk, qs, qk = refs[:6]
    sends, refs = refs[6 : 6 + pieces], refs[6 + pieces :]
    x, bg, act_n, eg_n, act_t, eg_t, sem_in = refs[:7]
    refs = refs[7:]
    scratch = [refs[5 * n : 5 * n + 5] for n in range(shards)]
    rows, width = toks[0].shape
    hidden = act_t.shape[0] // shards
    loads = []
    for n, tok in enumerate(toks):
        dst = (x, bg)[n % 2].at[pl.ds(n // 2 * rows, rows)]
        loads.append(pltpu.make_async_copy(tok, dst, sem_in.at[n]))
    weights = []
    for n, (we, ws, sem, bias_rows, sem_b) in enumerate(scratch):
        copies = load_weights(sources[n], we, ws, sem)
        if n:
            strip = width // chips
            copies.append(
                pltpu.make_async_copy(sources[n][0].at[pl.ds(strip, BIAS_ROWS)], bias_rows, sem_b)
            )
        weights.append(copies)
    for copy in loads + [c for copies in weights for c in copies]:
        copy.start()
    for copy in loads:
        copy.wait()
    step = min(256, hidden)
    for n, (we, ws, _, bias_rows, _) in enumerate(scratch):
        for copy in weights[n]:
            copy.wait()
        if n:
            bias = jnp.sum(bias_rows[:, :hidden].astype(F32), axis=0, keepdims=True)
        else:
            bias = bias_ref[:, pl.ds(pl.multiple_of(places()[0] * hidden, 128), hidden)]
        for h in range(0, hidden, step):
            block = slice(h, h + step)
            there = slice(n * hidden + h, n * hidden + h + step)
            v = nn(x[...], we[:, block]) + bias[:, block]
            square = v * v
            t = jnp.tanh(0.7978845608 * v * (1.0 + 0.044715 * square))
            low = 0.5 * (1.0 + t)
            slope = low + 0.5 * v * (1.0 - t * t) * (0.7978845608 * (1.0 + 0.134145 * square))
            act = (v * low).astype(BF)
            eg = (nt(bg[...], ws[block, :]) * slope).astype(BF)
            act_n[:, there] = act
            eg_n[:, there] = eg
            act_t[there, :] = act.T
            eg_t[there, :] = eg.T
            sums[n : n + 1, block] = jnp.sum(eg.astype(F32), axis=0, keepdims=True)
    step = min(256, width)
    for c in range(0, width, step):
        block = slice(c, c + step)
        grad, out = 0.0, 0.0
        for n, (we, ws, _, _, _) in enumerate(scratch):
            part = slice(n * hidden, (n + 1) * hidden)
            grad = grad + nt(eg_n[:, part], we[block, :])
            out = out + nn(act_n[:, part], ws[:, block])
        for m, value in enumerate((grad, out)):
            for r in range(4):
                place, dst = (m, r // 2), keep
                if r % 2:
                    flat = 2 * m + r // 2
                    dst = sends[flat * pieces // 4]
                    place = {1: place, 2: place[1:], 4: ()}[pieces]
                dst[(*place, slice(None), block)] = value[r * rows : (r + 1) * rows].astype(BF)
    chunk = width // chips
    half = chunk // 2
    core, chip, _ = places()
    top = chips.bit_length() - 2

    def store(dst, i, tile, turned):
        for n in range(shards):
            for a in range(2):
                part = tile[n * hidden : (n + 1) * hidden, a * half : (a + 1) * half]
                dst[i, n, core ^ a] = part.T if turned else part

    for left, right, bit, go, stay in ((eg_t, x, 0, ps, pk), (act_t, bg, top, qs, qk)):
        for dst, js in ((go, with_bit(chips, bit)), (stay, without_bit(chips, bit))):
            for i, j in enumerate(js):
                if half % 128 == 0:
                    start = pl.multiple_of((chip ^ j) * chunk, 128)
                    store(dst, i, nn(left[...], right[:, pl.ds(start, chunk)]).astype(BF), False)
                    continue
                for k in range(chips):

                    @pl.when(chip ^ j == k)
                    def narrow():
                        span = slice(k * chunk, (k + 1) * chunk)
                        store(dst, i, nn(left[...], right[:, span]).astype(BF), True)


def feed(chips, toks, sources, bias, hidden, after=()):
    rows, width = toks[0].shape
    shards = len(sources)
    half = width // chips // 2
    edge = (hidden, half) if half % 128 == 0 else (half, hidden)
    piece = struct((chips // 2, shards, 2, *edge), BF)
    scratch = [pltpu.VMEM((4 * rows, width), BF)] * 2
    scratch += [pltpu.VMEM((4 * rows, shards * hidden), BF)] * 2
    scratch += [pltpu.VMEM((shards * hidden, 4 * rows), BF)] * 2
    scratch += [pltpu.SemaphoreType.DMA((8,))]
    for _ in range(shards):
        scratch += weight_scratch(chips, hidden, width)
        scratch += [pltpu.VMEM((BIAS_ROWS, 2 * hidden), BF), pltpu.SemaphoreType.DMA(())]
    args = (*toks, *[a for source in sources for a in source])
    specs = {n: ANY for n in range(len(args))}
    result = struct((2, 2, rows, width), BF)
    return call(
        partial(feed_kernel, chips, shards, CFG["send"]),
        (*args, bias),
        (struct((shards, hidden), F32), result)
        + (piece,) * 4
        + (struct({1: (2, 2, rows, width), 2: (2, rows, width), 4: (rows, width)}[CFG["send"]], BF),)
        * CFG["send"],
        scratch=scratch,
        specs=specs,
        vmem=36,
        tag="M",
        after=after,
    )


def norm_back_kernel(spot, info, x_ref, u_ref, gain_ref, g0, g1, g2, g3, sum_ref, biases, out_ref, small_ref):
    rows, width = x_ref.shape
    step = 64
    count = info[COUNT : COUNT + 1, 0:1].astype(F32)
    gain_sum = jnp.zeros((1, width), F32)
    shift_sum = jnp.zeros((1, width), F32)
    for r in range(0, rows, step):
        here = slice(r, r + step)
        xhat, inverse = normalize(x_ref[here, :].astype(F32))
        grad = g0[here, :] + g1[0, 0, here, :].astype(F32) + g2[(*spot, here)].astype(F32)
        grad = grad + g3[0, here, :].astype(F32)
        gain_sum = gain_sum + jnp.sum(grad * xhat, axis=0, keepdims=True)
        shift_sum = shift_sum + jnp.sum(grad, axis=0, keepdims=True)
        scaled = grad * gain_ref[...]
        mean = jnp.mean(scaled, axis=-1, keepdims=True)
        dot = jnp.mean(scaled * xhat, axis=-1, keepdims=True)
        out_ref[here, :] = u_ref[here, :].astype(F32) * count + inverse * (
            scaled - mean - xhat * dot
        )
    small_ref[...] = jnp.zeros(small_ref.shape, F32)
    small_ref[0:1, :] = gain_sum
    small_ref[1:2, :] = shift_sum
    small_ref[2:3, :] = sum_ref[...]
    small_ref[3:4, :] = jnp.zeros((1, width), F32) + count
    shards, hidden = biases.shape
    half = pl.ds(pl.multiple_of(places()[0] * hidden, 128), hidden)
    small_ref[SUMS : SUMS + shards, half] = biases[...]


def norm_back(info, x, u, gain, g0, g1, g2, g3, sums, biases, after=()):
    small = (SUMS + biases.shape[0], x.shape[1])
    return call(
        partial(norm_back_kernel, g2[1]),
        (info, x, u, gain, g0, g1, g2[0], g3, sums, biases),
        (struct(x.shape, F32), struct(small, F32)),
        after=after,
        tag="nb",
    )


def small_kernel(axis, bit, mine, other, out):
    if axis == "dp":
        out[...] = mine[...] + other[...]
        return
    out[:SUMS, :] = mine[:SUMS, :] + other[:SUMS, :]
    step = (1 << bit) // 2
    for k in range(mine.shape[0] - SUMS):
        row = slice(SUMS + k, SUMS + k + 1)
        if step and not k & step:
            twin = SUMS + (k | step)
            out[row, :] = mine[row, :] + other[twin : twin + 1, :]
        else:
            out[row, :] = mine[row, :]


def small_sum(small, axis, bit):
    other = exchange(small, axis, 1 << bit)
    return call(partial(small_kernel, axis, bit), (small, other), struct(small.shape, F32), tag="sm")


def row_out_kernel(spot, info, x_ref, sum_ref, g1, g2, g3, bias_ref, out_ref):
    rows, width = x_ref.shape
    step = 64
    for r in range(0, rows, step):
        here = slice(r, r + step)
        branch = sum_ref[here, :] + g1[1, 0, here, :].astype(F32) + g2[(*spot, here)].astype(F32)
        branch = branch + g3[g3.shape[0] - 1, here, :].astype(F32) + bias_ref[...]
        where = lax.broadcasted_iota(jnp.int32, (step, width), 0) + r
        branch = jnp.where(where < info[LIVE : LIVE + 1, 0:1], branch, 0.0)
        out_ref[here, :] = (x_ref[here, :].astype(F32) + branch).astype(BF)


def row_out(info, x, attention_out, g1, g2, g3, bias, after=()):
    return call(
        partial(row_out_kernel, g2[1]),
        (info, x, attention_out, g1, g2[0], g3, bias),
        struct(x.shape, BF),
        after=after,
        tag="ro",
    )


def attend_final_kernel(scale, picks, small_ref, *refs):
    parts, (attend, output) = refs[:-2], refs[-2:]
    depth = len(picks)
    cols = parts[0].shape[2]
    edge = 3 * depth // 4
    factor = scale / small_ref[3:4, 0:1]
    for j, (n, index) in picks.items():
        place = places()[2] ^ j
        value = parts[n][index].astype(F32) * factor

        @pl.when(place < edge)
        def inner():
            attend[:, pl.ds(pl.multiple_of(place * cols, 128), cols)] = value

        @pl.when(place >= edge)
        def outer():
            output[:, pl.ds(pl.multiple_of((place - edge) * cols, 128), cols)] = value


def attend_final(scale, small, have):
    arrays, picks = [], {}
    for j, (array, index) in have.items():
        n = next((n for n, a in enumerate(arrays) if a is array), len(arrays))
        if n == len(arrays):
            arrays.append(array)
        picks[j] = (n, index)
    _, half, cols = arrays[0].shape
    depth = len(picks)
    attend, output = (half, 3 * depth // 4 * cols), (half, depth // 4 * cols)
    return call(
        partial(attend_final_kernel, scale, picks),
        (small, *arrays),
        (struct(attend, F32), struct(output, F32)),
        tag="af",
    )


def row_final_kernel(scale, small_ref, grad_ref, out_ref, gain, shift, bias, expand):
    factor = scale / small_ref[3:4, 0:1]
    out_ref[...] = grad_ref[...] * factor
    gain[...] = small_ref[0:1, :] * factor
    shift[...] = small_ref[1:2, :] * factor
    bias[...] = small_ref[2:3, :] * factor
    expand[...] = small_ref[SUMS : SUMS + 1, : expand.shape[1]] * factor


def row_final(scale, small, grad, shard):
    row = struct((1, grad.shape[1]), F32)
    return call(
        partial(row_final_kernel, scale),
        (small, grad),
        (struct(grad.shape, F32), row, row, row, struct((1, shard), F32)),
        tag="rf",
    )


def feed_final_kernel(scale, narrow, small_ref, mine, sibling, expand, shrink):
    hidden = mine.shape[2 if narrow else 1]
    factor = scale / small_ref[3:4, 0:1]
    for n, part in enumerate((mine, sibling)):
        start = pl.multiple_of((places()[0] ^ n) * hidden, 128)
        first, second = part[0].astype(F32), part[1].astype(F32)
        expand[:, pl.ds(start, hidden)] = (first if narrow else first.T) * factor
        shrink[pl.ds(start, hidden), :] = (second.T if narrow else second) * factor


def feed_final(scale, small, mine, sibling, half):
    narrow = half % 128 != 0
    hidden = mine.shape[2 if narrow else 1]
    return call(
        partial(feed_final_kernel, scale, narrow),
        (small, mine, sibling),
        (struct((half, 2 * hidden), F32), struct((2 * hidden, half), F32)),
        tag="ff",
    )


def add_kernel(plan, *refs):
    ins = refs[: len(refs) - len(plan)]
    for out, (_, parts) in zip(refs[len(ins) :], plan):
        for p, part in enumerate(parts):
            out[p] = sum(ins[n][index].astype(F32) for n, index in part).astype(out.dtype)


def add(plan, tag, after=()):
    arrays, outs, inner = [], [], []
    for dtype, parts in plan:
        entries = []
        for part in parts:
            entry = []
            for array, index in part:
                n = next((n for n, a in enumerate(arrays) if a is array), len(arrays))
                if n == len(arrays):
                    arrays.append(array)
                entry.append((n, index))
            entries.append(entry)
        inner.append((dtype, entries))
        array, index = parts[0][0]
        outs.append(struct((len(parts), *array.shape[len(index) :]), dtype))
    return call(partial(add_kernel, inner), tuple(arrays), tuple(outs), tag=tag, after=after)


def exchange(x, axis, flip):
    n = lax.axis_size(axis)
    return lax.ppermute(x, axis, [(i, i ^ flip) for i in range(n)])


def reduce_chips(chips, low, high, tag, afters=()):
    bits = list(range(chips.bit_length() - 1))
    orders = (bits, bits[::-1])
    left = []
    for (send, keep), order in zip((low, high), orders):
        got = exchange(send, "dp", 2 << order[0])
        left.append([[(keep, (i,)), (got, (i,))] for i in range(chips // 2)])
    sends = ()
    for n in range(1, len(bits)):
        stay, go = [], []
        for entries, order in zip(left, orders):
            if order[0] == 0:
                stay.append(entries[0::2])
                go.append(entries[1::2])
            else:
                stay.append(entries[: len(entries) // 2])
                go.append(entries[len(entries) // 2 :])
        sends = add([(BF, g) for g in go], tag, after=afters)
        left = []
        for entries, send, order in zip(stay, sends, orders):
            got = exchange(send, "dp", 2 << order[n])
            left.append([e + [(got, (i,))] for i, e in enumerate(entries)])
    return (left[0][0], left[1][0]), sends


def behind(x, *others):
    return lax.optimization_barrier((x, *others))[0]


def reduce_depth(parts, entries, depth):
    left = {j: e for j, e in enumerate(entries)}
    for bit in range(depth.bit_length() - 1):
        go = [j for j in left if j >> bit & 1]
        if bit:
            parts = add([(BF, [left[j] for j in go])], "zadd")[0]
        got = exchange(parts, "mp", 1 << bit)
        for n, j in enumerate(go):
            left[j ^ (1 << bit)] = left[j ^ (1 << bit)] + [(got, (n,))]
            del left[j]
    return left[0]


def gather_depth(own, depth):
    have = {0: (own, (0,))}
    packed = own
    for bit in reversed(range(depth.bit_length() - 1)):
        order = list(have)
        if len(order) > 1:
            packed = add([(BF, [[have[j]] for j in order])], "zjoin")[0]
        got = exchange(packed, "mp", 1 << bit)
        for n, j in enumerate(order):
            have[j ^ (1 << bit)] = (got, (n,))
    return have


def at(entry, *index):
    return [(array, first + index) for array, first in entry]


def local(
    residual_in,
    upstream,
    layer_norm_gain,
    layer_norm_bias,
    attend_weight,
    output_weight,
    expand_weight,
    expand_bias,
    shrink_weight,
    shrink_bias,
    seq_lengths,
    terminal_pos,
    window_offset,
):
    rows, width = residual_in.shape
    data_ways, depth = lax.axis_size("dp"), lax.axis_size("mp")
    chips = data_ways // 2
    shards = depth // 2
    shard = expand_weight.shape[1]
    hidden = shard // 2
    gain = layer_norm_gain[None, :]
    packed = pack(chips, expand_bias[None, :], expand_weight, shrink_weight)
    shares = [exchange(packed, "mp", 2 * k) for k in range(1, shards)]
    info, normed, bg, shrink_bias_grad = prepare(
        seq_lengths,
        terminal_pos,
        window_offset,
        residual_in,
        upstream,
        gain,
        layer_norm_bias[None, :],
        after=(packed,),
    )
    tok = (normed, bg)
    tok_core = [exchange(t, "dp", 1) for t in tok]

    sides = attention(info, normed, bg, attend_weight, output_weight)
    grad_attention, attention_out = attention_back(sides, attend_weight, output_weight)
    deep_normed = exchange(behind(normed, sides) if CFG["deep0"] else normed, "mp", 1)
    wait = []
    if CFG["sidesB"]:
        wait.append(grad_attention)
    if CFG["sidesS"]:
        wait += shares
    if CFG["sidesC"]:
        wait += tok_core
    if CFG["sidesD"]:
        wait.append(deep_normed)
    sides_core = exchange(behind(sides, *wait) if wait else sides, "dp", 1)
    hold = {0: (), 1: (sides,), 2: (deep_normed,), 3: (grad_attention,), 4: tuple(shares)}[CFG["deep1"]]
    tok_deep = [deep_normed, exchange(behind(bg, *hold) if hold else bg, "mp", 1)]
    hold = {0: (), 1: (sides,), 2: (grad_attention,), 3: (sides_core,)}[CFG["W2"]]
    held = [behind(s, *hold) if hold else s for s in shares]
    foreign = [[s] + [exchange(s, "dp", 2 * j) for j in range(1, chips)] for s in held]
    attn = attention_grads(
        chips, depth, tok, tok_core, sides, sides_core, after={0: (), 1: shares, 2: (*shares, grad_attention)}[CFG["A3S"]]
    )
    hold = {0: (), 1: (attn[0],), 2: (sides,), 3: (sides_core,)}[CFG["bothA3"]]
    tok_both = [exchange(behind(t, *hold) if hold else t, "dp", 1) for t in tok_deep]
    if CFG["attnBoth"]:
        attn = [behind(a, *tok_both) for a in attn]
    toks = (*tok, *tok_core, *tok_deep, *tok_both)

    fed = feed(
        chips,
        toks,
        [(expand_weight, shrink_weight), *foreign],
        expand_bias[None, :],
        hidden,
        after=attn[:1] if CFG["MA3"] else (),
    )
    sums, keep = fed[:2]
    got = [exchange(f, "dp", 1) for f in fed[6:]]

    def passed(m, r):
        return {1: (got[0], (m, r)), 2: (got[m % len(got)], (r,)), 4: (got[-1 if len(got) < 4 else 2 * m + r], ())}[len(got)]

    entries = [[(keep, (m, 1)), passed(m, 1)] for m in range(2)]
    if CFG["cross2"]:
        crossing = add([(BF, [e]) for e in entries], "cross")
        crossed = [exchange(c, "mp", 1) for c in crossing]
    else:
        crossing = add([(BF, entries)], "cross")
        crossed = [exchange(crossing[0], "mp", 1)]

    hold = {0: (), 1: (keep,), 2: (crossing[0],)}[CFG["at1"]]
    tracks, attn_sent = reduce_chips(chips, attn[:2], attn[2:], "at1", hold)
    middle = depth // 2
    entries = [at(tracks[z // middle], z % middle) for z in range(depth)]

    def feed_sums():
        hold = {0: (), 1: (attn_sent[0],), 2: (crossing[0],), 3: (attn_sent[0], crossing[0])}[CFG["fo1"]]
        return reduce_chips(chips, fed[2:4], fed[4:6], "fo1", hold)

    def rows_back(after):
        return norm_back(
            info,
            residual_in,
            upstream,
            gain,
            grad_attention,
            keep,
            passed(0, 0),
            crossed[0],
            shrink_bias_grad,
            sums,
            after=after,
        )

    def attention_parts(after):
        return add([(BF, [e for j, e in enumerate(entries) if j & 1])], "parts", after=after)

    mine, away = [[], []], [[], []]
    if CFG["nb"] == 1:
        grad_rows, small = rows_back(())
    if CFG["first"]:
        parts = attention_parts((small,) if CFG["nb"] == 1 and CFG["parts"] else ())
        pair, sent = feed_sums()
    else:
        pair, sent = feed_sums()
        parts = attention_parts({0: (), 1: (sent[0],), 2: (small,) if CFG["nb"] == 1 else ()}[CFG["parts"]])
    if CFG["nb"] != 1:
        grad_rows, small = rows_back((parts[0],) if CFG["nb"] else ())
    hold = {0: (), 1: (parts[0],), 2: (small,)}[CFG["both"]]
    for k in range(1, shards):
        both = add([(BF, [at(p, k, a) for p in pair for a in range(2)])], "both", after=hold)[0]
        both = exchange(both, "mp", 2 * k)
        for n in range(2):
            mine[n].append((both, (2 * n,)))
            away[n].append((both, (2 * n + 1,)))
    if CFG["nb"] == 3:
        pass
    attn_own = add([(BF, [reduce_depth(parts[0], entries, depth)])], "aown")[0]
    attn_all = gather_depth(attn_own, depth)
    for n in range(2):
        mine[n] += at(pair[n], 0, 0)
        away[n] += at(pair[n], 0, 1)
    mine, away = add([(F32, mine), (BF, away)], "mine")
    sibling = exchange(away, "dp", 1)

    residual_out = row_out(
        info, residual_in, attention_out, keep, passed(1, 0), crossed[-1], shrink_bias[None, :]
    )
    for bit in range(depth.bit_length() - 1):
        small = small_sum(small, "mp", bit)
    for bit in range(data_ways.bit_length() - 1):
        small = small_sum(small, "dp", bit)

    factor = float(data_ways * depth)
    attend_sum, output_sum = attend_final(factor, small, attn_all)
    expand_sum, shrink_sum = feed_final(factor, small, mine, sibling, width // data_ways)
    grad_rows, gain_sum, shift_sum, bias_sum, expand_bias_sum = row_final(
        factor, small, grad_rows, shard
    )
    return (
        residual_out,
        grad_rows,
        gain_sum[0],
        shift_sum[0],
        attend_sum,
        output_sum,
        expand_sum,
        expand_bias_sum[0],
        shrink_sum,
        bias_sum[0],
    )


def solution(mesh):
    in_specs = (
        P(("dp", "mp"), None),
        P(("dp", "mp"), None),
        P(),
        P(),
        P(),
        P(),
        P(None, "mp"),
        P("mp"),
        P("mp", None),
        P(),
        P("dp", None),
        P("dp", "mp"),
        P("dp", "mp"),
    )
    out_specs = (
        P(("dp", "mp"), None),
        P(("dp", "mp"), None),
        P(),
        P(),
        P("dp", None),
        P("dp", None),
        P("dp", "mp"),
        P("mp"),
        P("mp", "dp"),
        P(),
    )
    return jax.shard_map(local, mesh=mesh, in_specs=in_specs, out_specs=out_specs, check_vma=False)
```
